32 devices in a mesh: vocab: 8 (over z, y), section: 4 (over x, core).
Axes of the slice: x: 2, y: 2, z: 4, core: 2. Of those that a mesh axis runs over, the one named last changes fastest.
Arguments:
- hidden: bfloat16 [4, 32, 8192], P('section', 'vocab'), may hold values from -64 to 64
- policy_head: bfloat16 [9504, 8192], P(('vocab', 'section')), may hold values from -1 to 1
- reference_head: bfloat16 [9504, 8192], P(('vocab', 'section')), may hold values from -1 to 1
- targets: int32 [4, 32], replicated, may hold values from 0 to 9503
- loss_mask: int32 [4, 32], replicated, may hold values 0 or 1
Outputs:
- token_logprob: float32 [4, 32], replicated
- token_kl: float32 [4, 32], replicated
- totals: float32 [3], replicated
The draws below stay inside these ranges and needn't reach their ends.
All inputs are finite; a program needn't handle non-finite values.
Results may differ from the reference program's by a relative error of at most 0.0003.
Values may be sent and summed in bfloat16 or wider, within the bound.
A program may use at most 128 MiB of HBM per device.

```python
import jax
import jax.numpy as jnp
from jax import lax

D = 8192
VOCAB = 9504
TOK_MB = 32
MICRO = 4


def head_row(key, salt, index):
    base = jax.random.fold_in(jax.random.fold_in(key, salt), index)
    return jax.random.truncated_normal(base, -6.0, 6.0, (D,), jnp.float32) * D ** (-0.5)


def head_rows(key, salt):
    indices = jnp.arange(VOCAB, dtype=jnp.int32)
    return jax.vmap(lambda index: head_row(key, salt, index))(indices)


def draw_policy_head(key, part):
    return head_rows(key, 11).astype(jnp.bfloat16)


def draw_reference_head(key, part):
    return (head_rows(key, 11) + 0.6 * head_rows(key, 12)).astype(jnp.bfloat16)


def draw_hidden(key, part):
    values = jax.random.truncated_normal(jax.random.fold_in(key, 21), -6.0, 6.0, (MICRO, TOK_MB, D), jnp.float32)
    return values.astype(jnp.bfloat16)


def touch_ends(values, stream_key, smallest, high):
    longest = values.shape.index(max(values.shape))
    spots = []
    for shift in (0, 1):
        where = [jax.random.randint(jax.random.fold_in(stream_key, axis), (), 0, length) for axis, length in enumerate(values.shape)]
        where[longest] = (where[longest] + shift) % values.shape[longest]
        spots.append(tuple(where))
    return values.at[spots[0]].set(smallest).at[spots[1]].set(high)


def setup_inputs(seed: int = 0) -> dict:
    streams_of = jax.random.split(jax.random.key(seed), 6)
    return {
        "hidden": draw_hidden(jax.random.fold_in(streams_of[5], 71), 0),
        "policy_head": draw_policy_head(jax.random.fold_in(streams_of[5], 71), 0),
        "reference_head": draw_reference_head(jax.random.fold_in(streams_of[5], 71), 0),
        "targets": touch_ends(jax.random.randint(streams_of[3], (MICRO, TOK_MB), 0, VOCAB), jax.random.fold_in(streams_of[3], 1), 0, VOCAB - 1).astype(jnp.int32),
        "loss_mask": touch_ends((jax.random.randint(streams_of[4], (MICRO, TOK_MB), 0, 4) < 3).astype(jnp.int32), jax.random.fold_in(streams_of[4], 1), 0, 1),
    }


def log_norm(logits):
    largest = jnp.max(logits, axis=1, keepdims=True)
    return largest[:, 0] + jnp.log(jnp.sum(jnp.exp(logits - largest), axis=1))


def micro_batch(inputs, policy_head, reference_head):
    hidden_rows, target = inputs
    contract_dims = (((1,), (1,)), ((), ()))
    policy_logits = lax.dot_general(hidden_rows, policy_head, contract_dims, preferred_element_type=jnp.float32)
    refer_logits = lax.dot_general(hidden_rows, reference_head, contract_dims, preferred_element_type=jnp.float32)
    policy_lse = log_norm(policy_logits)
    refer_lse = log_norm(refer_logits)
    policy_probs = jnp.exp(policy_logits - policy_lse[:, None])
    chosen = jnp.take_along_axis(policy_logits, target[:, None].astype(jnp.int32), axis=1)[:, 0]
    logprob = chosen - policy_lse
    entropy = policy_lse - jnp.sum(policy_probs * policy_logits, axis=1)
    divergence = jnp.sum(policy_probs * (policy_logits - refer_logits), axis=1) - policy_lse + refer_lse
    return logprob, entropy, divergence


def reference(hidden, policy_head, reference_head, targets, loss_mask):
    logprob, entropy, divergence = lax.map(lambda inputs: micro_batch(inputs, policy_head, reference_head), (hidden, targets))
    weights = loss_mask.astype(jnp.float32)
    scale = 1.0 / (hidden.shape[0] * hidden.shape[1])
    totals = jnp.stack([jnp.sum(weights * logprob), jnp.sum(weights * entropy), jnp.sum(weights * divergence)]) * scale
    return logprob, divergence, totals
```

```python
import functools
import itertools

import jax
import jax.numpy as jnp
from jax import lax
from jax.experimental import pallas as pl
from jax.experimental.pallas import tpu as pltpu
from jax.sharding import PartitionSpec as P

MESH = pl.DeviceIdType.MESH


def split_axis(size):
    return (size // 2, 2) if size % 2 == 0 else (size, 1)


def power_of_two(size):
    return size & (size - 1) == 0


def flip(index, step, size):
    result = index
    bit = 1
    while bit < size:
        if step & bit:
            result = result + bit - 2 * bit * ((index // bit) % 2)
        bit *= 2
    return result


def target_of(index, step, size):
    if step == 0:
        return index
    return flip(index, step, size) if power_of_two(size) else (index + step) % size


def source_of(index, step, size):
    if step == 0:
        return index
    return flip(index, step, size) if power_of_two(size) else (index + size - step) % size


def merge(parts):
    tops = [part[0:1] for part in parts]
    rtops = [part[1:2] for part in parts]
    top = functools.reduce(jnp.maximum, tops)
    rtop = functools.reduce(jnp.maximum, rtops)
    total = first = cross = chosen = rtotal = 0.0
    for part in parts:
        shift = part[0:1] - top
        scale = jnp.exp(shift)
        total = total + scale * part[2:3]
        first = first + scale * (part[3:4] + shift * part[2:3])
        cross = cross + scale * part[4:5]
        chosen = chosen + part[5:6]
        rtotal = rtotal + jnp.exp(part[1:2] - rtop) * part[6:7]
    return top, rtop, total, first, cross, chosen, rtotal


def kernel(
    sizes, hid, hp, hr, tgt, msk, out_lp, out_kl, out_tot,
    blocks, rows, wp, wr, plane, line, local_sem, send_sem, recv_sem,
):
    vocab, section = sizes
    A, B = split_axis(vocab)
    X, C = split_axis(section)
    v, s = lax.axis_index("vocab"), lax.axis_index("section")
    a, b = v // B, v % B
    x, c = s // C, s % C
    dims = (A, B, X, C)
    here = (a, b, x, c)
    piece, width = hid.shape[1], hid.shape[2]
    tokens = rows.shape[0]
    micro, span = tgt.shape
    count = wp.shape[0]

    def device(at):
        return (at[0] * B + at[1], at[2] * C + at[3])

    def slot(at):
        return (at[2] * C + at[3]) * vocab + at[0] * B + at[1]

    def to(step):
        return tuple(target_of(i, d, n) for i, d, n in zip(here, step, dims))

    def back(step):
        return tuple(source_of(i, d, n) for i, d, n in zip(here, step, dims))

    own = pltpu.make_async_copy(hid.at[0], blocks.at[slot(here)], local_sem.at[0])
    own.start()
    load_p = pltpu.make_async_copy(hp, wp, local_sem.at[1])
    load_p.start()
    load_r = pltpu.make_async_copy(hr, wr, local_sem.at[2])
    load_r.start()

    line_steps = [(d, 0, 0, 0) for d in range(1, A)]
    plane_steps = [(0,) + e for e in itertools.product(range(B), range(X), range(C)) if any(e)]
    barrier = pltpu.get_barrier_semaphore()
    for step in line_steps + plane_steps:
        pl.semaphore_signal(barrier, inc=1, device_id=device(to(step)), device_id_type=MESH)
    pl.semaphore_wait(barrier, len(line_steps) + len(plane_steps))
    own.wait()

    keys = {}
    sent = []

    def view(at, half):
        ref = blocks.at[slot(at)]
        if half is None:
            return ref
        return ref.at[:, pl.ds(half * (width // 2), width // 2)]

    def copy(key, step, at, half=None):
        i = keys.setdefault(key, len(keys))
        part = view(at, half)
        op = pltpu.make_async_remote_copy(
            src_ref=part, dst_ref=part, send_sem=send_sem.at[i], recv_sem=recv_sem.at[i],
            device_id=device(to(step)), device_id_type=MESH,
        )
        op.start()
        sent.append(op)

    def arrive(key, step, at, half=None):
        i = keys.setdefault(key, len(keys))
        part = view(at, half)
        pltpu.make_async_remote_copy(
            src_ref=part, dst_ref=part, send_sem=send_sem.at[i], recv_sem=recv_sem.at[i],
            device_id=device(to(step)), device_id_type=MESH,
        ).wait_recv()

    def to_cores(step):
        for dc in range(1, C):
            copy(("core", step, dc), (0, 0, 0, dc), back(step))

    for step in line_steps:
        copy(("line", step), step, here)

    def fan(d):
        at = back((d, 0, 0, 0))
        for dx in range(1, X):
            copy(("x", d, dx), (0, 0, dx, 0), at)
        for db in range(1, B):
            copy(("b", d, db), (0, db, 0, 0), at)
        to_cores((d, 0, 0, 0))

    def cross(d):
        for dx in range(1, X):
            at = back((d, 0, dx, 0))
            arrive(("x", d, dx), (0, 0, dx, 0), at)
            for db in range(1, B):
                copy(("xb", d, dx, db), (0, db, 0, 0), at, 0)
        for db in range(1, B):
            at = back((d, db, 0, 0))
            arrive(("b", d, db), (0, db, 0, 0), at)
            for dx in range(1, X):
                copy(("bx", d, dx, db), (0, 0, dx, 0), at, 1)
        for dx in range(1, X):
            to_cores((d, 0, dx, 0))
        for db in range(1, B):
            to_cores((d, db, 0, 0))

    def corner(d):
        for dx in range(1, X):
            for db in range(1, B):
                at = back((d, db, dx, 0))
                arrive(("xb", d, dx, db), (0, db, 0, 0), at, 0)
                arrive(("bx", d, dx, db), (0, 0, dx, 0), at, 1)
                to_cores((d, db, dx, 0))

    for d in range(A + 2):
        if d < A:
            if d:
                arrive(("line", (d, 0, 0, 0)), (d, 0, 0, 0), back((d, 0, 0, 0)))
            fan(d)
        if 1 <= d < A + 1:
            cross(d - 1)
        if d >= 2:
            corner(d - 2)
    for d in range(A):
        for db, dx in itertools.product(range(B), range(X)):
            for dc in range(1, C):
                arrive(("core", (d, db, dx, 0), dc), (0, 0, 0, dc), back((d, db, dx, dc)))

    bundle = 16 // piece if piece < 16 and 16 % piece == 0 and blocks.shape[0] % (16 // piece) == 0 else 1
    high = bundle * piece

    def pack(i, carry):
        base = pl.multiple_of(i * high, high)
        rows[pl.ds(base, high), :] = jnp.concatenate(
            [blocks[i * bundle + j] for j in range(bundle)], axis=0
        )
        return carry

    lax.fori_loop(0, blocks.shape[0] // bundle, pack, 0)
    load_p.wait()
    load_r.wait()

    wanted = jnp.concatenate([tgt[i : i + 1, :] for i in range(micro)], axis=1)
    offset = (v * section + s) * count
    tile = 128 if tokens % 128 == 0 else tokens
    dims_nt = (((1,), (1,)), ((), ()))
    index = b * (X * C) + x * C + c
    moments = []
    for n in range(tokens // tile):
        mine = rows[n * tile : (n + 1) * tile, :]
        plog = lax.dot_general(wp[...], mine, dims_nt, preferred_element_type=jnp.float32)
        rlog = lax.dot_general(wr[...], mine, dims_nt, preferred_element_type=jnp.float32)
        top = jnp.max(plog, axis=0, keepdims=True)
        shift = plog - top
        weight = jnp.exp(shift)
        total = jnp.sum(weight, axis=0, keepdims=True)
        first = jnp.sum(weight * shift, axis=0, keepdims=True)
        across = jnp.sum(weight * (plog - rlog), axis=0, keepdims=True)
        ids = offset + lax.broadcasted_iota(jnp.int32, plog.shape, 0)
        chosen = jnp.sum(
            jnp.where(ids == wanted[:, n * tile : (n + 1) * tile], plog, 0.0), axis=0, keepdims=True
        )
        rtop = jnp.max(rlog, axis=0, keepdims=True)
        rtotal = jnp.sum(jnp.exp(rlog - rtop), axis=0, keepdims=True)
        moments.append(
            jnp.concatenate([top, rtop, total, first, across, chosen, rtotal, jnp.zeros_like(top)], axis=0)
        )
    plane[index] = jnp.concatenate(moments, axis=1) if len(moments) > 1 else moments[0]

    def share(kind, step, buffer, at, start):
        i = keys.setdefault((kind, step), len(keys))
        op = pltpu.make_async_remote_copy(
            src_ref=buffer.at[at], dst_ref=buffer.at[at],
            send_sem=send_sem.at[i], recv_sem=recv_sem.at[i],
            device_id=device(to(step)), device_id_type=MESH,
        )
        if start:
            op.start()
            sent.append(op)
        else:
            op.wait_recv()

    def plane_index(at):
        return at[1] * (X * C) + at[2] * C + at[3]

    for step in plane_steps:
        share("plane", step, plane, plane_index(here), True)
    for step in plane_steps:
        share("plane", step, plane, plane_index(back(step)), False)
    merged = merge([plane[i] for i in range(B * X * C)])
    line[a] = jnp.concatenate(list(merged) + [jnp.zeros_like(merged[0])], axis=0)
    for step in line_steps:
        share("stat", step, line, a, True)
    for step in line_steps:
        share("stat", step, line, back(step)[0], False)
    top, rtop, total, first, across, chosen, rtotal = merge([line[i] for i in range(A)])
    log_total = jnp.log(total)
    lse = top + log_total
    logprob = chosen - lse
    entropy = log_total - first / total
    divergence = across / total - lse + (rtop + jnp.log(rtotal))
    mask = jnp.concatenate([msk[i : i + 1, :] for i in range(micro)], axis=1).astype(jnp.float32)
    scale = 1.0 / (micro * span)
    out_tot[0] = jnp.sum(mask * logprob) * scale
    out_tot[1] = jnp.sum(mask * entropy) * scale
    out_tot[2] = jnp.sum(mask * divergence) * scale
    for i in range(micro):
        out_lp[i : i + 1, :] = logprob[:, i * span : (i + 1) * span]
        out_kl[i : i + 1, :] = divergence[:, i * span : (i + 1) * span]
    for op in sent:
        op.wait_send()


def on_device(sizes, hidden, policy_head, reference_head, targets, loss_mask):
    vocab, section = sizes
    A, B = split_axis(vocab)
    X, C = split_axis(section)
    piece, width = hidden.shape[1], hidden.shape[2]
    devices = vocab * section
    tokens = targets.size
    copies = (
        (A - 1) + A * (X - 1 + B - 1) + 2 * A * (X - 1) * (B - 1)
        + A * B * X * (C - 1) + (B * X * C - 1) + (A - 1)
    )
    anywhere = pl.BlockSpec(memory_space=pl.ANY)
    vmem = pl.BlockSpec(memory_space=pltpu.VMEM)
    heads = policy_head.size + reference_head.size
    return pl.pallas_call(
        functools.partial(kernel, sizes),
        out_shape=(
            jax.ShapeDtypeStruct(targets.shape, jnp.float32),
            jax.ShapeDtypeStruct(targets.shape, jnp.float32),
            jax.ShapeDtypeStruct((3,), jnp.float32),
        ),
        in_specs=[anywhere, anywhere, anywhere, vmem, vmem],
        out_specs=(vmem, vmem, pl.BlockSpec(memory_space=pltpu.SMEM)),
        scratch_shapes=[
            pltpu.VMEM((devices, piece, width), hidden.dtype),
            pltpu.VMEM((tokens, width), hidden.dtype),
            pltpu.VMEM(policy_head.shape, policy_head.dtype),
            pltpu.VMEM(reference_head.shape, reference_head.dtype),
            pltpu.VMEM((B * X * C, 8, tokens), jnp.float32),
            pltpu.VMEM((A, 8, tokens), jnp.float32),
            pltpu.SemaphoreType.DMA((3,)),
            pltpu.SemaphoreType.DMA((copies,)),
            pltpu.SemaphoreType.DMA((copies,)),
        ],
        compiler_params=pltpu.CompilerParams(
            collective_id=0, has_side_effects=True, vmem_limit_bytes=60 * 1024 * 1024
        ),
        cost_estimate=pl.CostEstimate(
            flops=2 * tokens * heads, bytes_accessed=2 * heads, transcendentals=3 * tokens * policy_head.shape[0]
        ),
    )(hidden, policy_head, reference_head, targets, loss_mask)


def solution(mesh):
    placed = (
        P("section", "vocab", None),
        P(("vocab", "section"), None),
        P(("vocab", "section"), None),
        P(),
        P(),
    )
    sizes = (mesh.shape["vocab"], mesh.shape["section"])
    return jax.shard_map(
        functools.partial(on_device, sizes),
        mesh=mesh, in_specs=placed, out_specs=(P(), P(), P()), check_vma=False,
    )
```

```python
import functools
import itertools

import jax
import jax.numpy as jnp
from jax import lax
from jax.experimental import pallas as pl
from jax.experimental.pallas import tpu as pltpu
from jax.sharding import PartitionSpec as P

MESH = pl.DeviceIdType.MESH


def split_axis(size):
    return (size // 2, 2) if size % 2 == 0 else (size, 1)


def power_of_two(size):
    return size & (size - 1) == 0


def flip(index, step, size):
    result = index
    bit = 1
    while bit < size:
        if step & bit:
            result = result + bit - 2 * bit * ((index // bit) % 2)
        bit *= 2
    return result


def target_of(index, step, size):
    if step == 0:
        return index
    return flip(index, step, size) if power_of_two(size) else (index + step) % size


def source_of(index, step, size):
    if step == 0:
        return index
    return flip(index, step, size) if power_of_two(size) else (index + size - step) % size


def merge(parts):
    tops = [part[0:1] for part in parts]
    rtops = [part[1:2] for part in parts]
    top = functools.reduce(jnp.maximum, tops)
    rtop = functools.reduce(jnp.maximum, rtops)
    total = first = cross = chosen = rtotal = 0.0
    for part in parts:
        shift = part[0:1] - top
        scale = jnp.exp(shift)
        total = total + scale * part[2:3]
        first = first + scale * (part[3:4] + shift * part[2:3])
        cross = cross + scale * part[4:5]
        chosen = chosen + part[5:6]
        rtotal = rtotal + jnp.exp(part[1:2] - rtop) * part[6:7]
    return top, rtop, total, first, cross, chosen, rtotal


PARTS = 2
STEPS = 4


def kernel(
    sizes, hid, hp, hr, tgt, out,
    blocks, wp, wr, plog_acc, rlog_acc, plane, line,
    local_sem, all_sent, core_sem, stat_sent, recv_sem, stat_sem,
):
    vocab, section = sizes
    A, B = split_axis(vocab)
    X, C = split_axis(section)
    v, s = lax.axis_index("vocab"), lax.axis_index("section")
    a, b = v // B, v % B
    x, c = s // C, s % C
    dims = (A, B, X, C)
    here = (a, b, x, c)
    piece, width = hid.shape[1], hid.shape[2]
    devices = blocks.shape[0]
    tokens = devices * piece
    micro = tgt.shape[0]
    count = wp.shape[0]
    share_width = width // PARTS
    step_width = share_width // STEPS
    tile = 128 if tokens % 128 == 0 and 128 % piece == 0 else tokens

    def device(at):
        return (at[0] * B + at[1], at[2] * C + at[3])

    def slot(at):
        return (at[2] * C + at[3]) * vocab + at[0] * B + at[1]

    def to(step):
        return tuple(target_of(i, d, n) for i, d, n in zip(here, step, dims))

    def back(step):
        return tuple(source_of(i, d, n) for i, d, n in zip(here, step, dims))

    line_steps = [(d, 0, 0, 0) for d in range(1, A)]
    plane_steps = [(0,) + e for e in itertools.product(range(B), range(X), range(C)) if any(e)]
    barrier = pltpu.get_barrier_semaphore()
    for step in line_steps + plane_steps:
        pl.semaphore_signal(barrier, inc=1, device_id=device(to(step)), device_id_type=MESH)

    own = pltpu.make_async_copy(hid.at[0], blocks.at[slot(here)], local_sem.at[0])
    own.start()
    load_p = pltpu.make_async_copy(hp, wp, local_sem.at[1])
    load_p.start()
    load_r = pltpu.make_async_copy(hr, wr, local_sem.at[2])
    load_r.start()
    plog_acc[...] = jnp.zeros_like(plog_acc)
    rlog_acc[...] = jnp.zeros_like(rlog_acc)
    own.wait()
    pl.semaphore_wait(barrier, len(line_steps) + len(plane_steps))

    keys = {}

    def view(at, h, half):
        lo, size = h * share_width, share_width
        if half is not None:
            size = share_width // 2
            lo = lo + half * size
        return blocks.at[slot(at), :, pl.ds(lo, size)]

    def describe(key, step, at, h, half):
        part = view(at, h, half)
        if key[0] == "core":
            arrived = core_sem.at[h]
        else:
            arrived = recv_sem.at[keys.setdefault((h,) + key, len(keys))]
        return pltpu.make_async_remote_copy(
            src_ref=part, dst_ref=part, send_sem=all_sent.at[0], recv_sem=arrived,
            device_id=device(to(step)), device_id_type=MESH,
        )

    def copy(key, step, at, h, half=None):
        describe(key, step, at, h, half).start()

    def arrive(key, step, at, h, half=None):
        describe(key, step, at, h, half).wait_recv()

    def to_cores(step, h):
        for dc in range(1, C):
            copy(("core", step, dc), (0, 0, 0, dc), back(step), h)

    def fan(h, d):
        at = back((d, 0, 0, 0))
        if d:
            arrive(("line", d), (d, 0, 0, 0), at, h)
        for dx in range(1, X):
            copy(("x", d, dx), (0, 0, dx, 0), at, h)
        for db in range(1, B):
            copy(("b", d, db), (0, db, 0, 0), at, h)
        to_cores((d, 0, 0, 0), h)

    def cross(h, d):
        for dx in range(1, X):
            at = back((d, 0, dx, 0))
            arrive(("x", d, dx), (0, 0, dx, 0), at, h)
            for db in range(1, B):
                copy(("xb", d, dx, db), (0, db, 0, 0), at, h, 0)
        for db in range(1, B):
            at = back((d, db, 0, 0))
            arrive(("b", d, db), (0, db, 0, 0), at, h)
            for dx in range(1, X):
                copy(("bx", d, dx, db), (0, 0, dx, 0), at, h, 1)
        for dx in range(1, X):
            to_cores((d, 0, dx, 0), h)
        for db in range(1, B):
            to_cores((d, db, 0, 0), h)

    def corner(h, d):
        for dx in range(1, X):
            for db in range(1, B):
                at = back((d, db, dx, 0))
                arrive(("xb", d, dx, db), (0, db, 0, 0), at, h, 0)
                arrive(("bx", d, dx, db), (0, 0, dx, 0), at, h, 1)
                to_cores((d, db, dx, 0), h)

    def from_cores(h):
        if C > 1:
            part = blocks.at[pl.ds(0, devices // C * (C - 1)), :, pl.ds(0, share_width)]
            pltpu.make_async_copy(part, part, core_sem.at[h]).wait()

    dims_nt = (((1,), (1,)), ((), ()))

    def multiply(k):
        columns = pl.ds(k * step_width, step_width)

        def tile_of(n):
            first = n * (tile // piece)
            mine = jnp.concatenate(
                [blocks[first + i, :, columns] for i in range(tile // piece)], axis=0
            )
            place = pl.ds(n * tile if isinstance(n, int) else pl.multiple_of(n * tile, tile), tile)
            plog_acc[:, place] += lax.dot_general(
                wp[:, columns], mine, dims_nt, preferred_element_type=jnp.float32
            )
            rlog_acc[:, place] += lax.dot_general(
                wr[:, columns], mine, dims_nt, preferred_element_type=jnp.float32
            )

        if tokens == tile:
            tile_of(0)
        else:
            pl.loop(0, tokens // tile)(tile_of)

    for h in range(PARTS):
        for d in range(1, A):
            copy(("line", d), (d, 0, 0, 0), here, h)

    units = [(h, d) for h in range(PARTS) for d in range(A)]
    work = []
    loaded = False
    for u in range(len(units) + 2):
        if u < len(units):
            fan(*units[u])
        if 1 <= u < len(units) + 1:
            cross(*units[u - 1])
        if u >= 2:
            corner(*units[u - 2])
        if u >= A + 2:
            if not loaded:
                load_p.wait()
                load_r.wait()
                loaded = True
            h, step = (u - A - 2) // A, (u - A - 2) % A
            if step == 0:
                from_cores(h)
                work += [h * STEPS + i for i in range(STEPS)]
            take = -(-len(work) // (A - step))
            for k in work[:take]:
                multiply(k)
            work = work[take:]
    if not loaded:
        load_p.wait()
        load_r.wait()
    from_cores(PARTS - 1)
    work += [(PARTS - 1) * STEPS + i for i in range(STEPS)]
    for k in work:
        multiply(k)

    wanted = jnp.concatenate([tgt[i : i + 1, :] for i in range(micro)], axis=1)
    offset = (v * section + s) * count
    moments = []
    for n in range(tokens // tile):
        place = slice(n * tile, (n + 1) * tile)
        plog, rlog = plog_acc[:, place], rlog_acc[:, place]
        top = jnp.max(plog, axis=0, keepdims=True)
        shift = plog - top
        weight = jnp.exp(shift)
        total = jnp.sum(weight, axis=0, keepdims=True)
        first = jnp.sum(weight * shift, axis=0, keepdims=True)
        across = jnp.sum(weight * (plog - rlog), axis=0, keepdims=True)
        ids = offset + lax.broadcasted_iota(jnp.int32, plog.shape, 0)
        chosen = jnp.sum(jnp.where(ids == wanted[:, place], plog, 0.0), axis=0, keepdims=True)
        rtop = jnp.max(rlog, axis=0, keepdims=True)
        rtotal = jnp.sum(jnp.exp(rlog - rtop), axis=0, keepdims=True)
        moments.append(
            jnp.concatenate([top, rtop, total, first, across, chosen, rtotal, jnp.zeros_like(top)], axis=0)
        )
    index = b * (X * C) + x * C + c
    plane[index] = jnp.concatenate(moments, axis=1) if len(moments) > 1 else moments[0]

    shared = []

    def share(step, buffer, at, start):
        i = keys.setdefault(("stat", step), len(keys)) - gather_keys
        op = pltpu.make_async_remote_copy(
            src_ref=buffer.at[at], dst_ref=buffer.at[at],
            send_sem=stat_sent.at[i], recv_sem=stat_sem.at[i],
            device_id=device(to(step)), device_id_type=MESH,
        )
        if start:
            op.start()
            shared.append(op)
        else:
            op.wait_recv()

    def plane_index(at):
        return at[1] * (X * C) + at[2] * C + at[3]

    gather_keys = len(keys)
    for step in plane_steps:
        share(step, plane, plane_index(here), True)
    if devices > 1:
        sent = blocks.at[pl.ds(0, devices - 1)]
        pltpu.make_async_copy(sent, sent, all_sent.at[0]).wait()
    for step in plane_steps:
        share(step, plane, plane_index(back(step)), False)
    merged = merge([plane[i] for i in range(B * X * C)])
    line[a] = jnp.concatenate(list(merged) + [jnp.zeros_like(merged[0])], axis=0)
    for step in line_steps:
        share(step, line, a, True)
    for step in line_steps:
        share(step, line, back(step)[0], False)
    merged = merge([line[i] for i in range(A)])
    out[...] = jnp.concatenate(list(merged) + [jnp.zeros_like(merged[0])], axis=0)
    for op in shared:
        op.wait_send()


def finish(stats, msk, out_lp, out_kl, out_tot):
    micro, span = msk.shape
    top, rtop, total, first, across, chosen, rtotal = [stats[i : i + 1, :] for i in range(7)]
    log_total = jnp.log(total)
    lse = top + log_total
    logprob = chosen - lse
    entropy = log_total - first / total
    divergence = across / total - lse + (rtop + jnp.log(rtotal))
    mask = jnp.concatenate([msk[i : i + 1, :] for i in range(micro)], axis=1).astype(jnp.float32)
    scale = 1.0 / (micro * span)
    out_tot[0] = jnp.sum(mask * logprob) * scale
    out_tot[1] = jnp.sum(mask * entropy) * scale
    out_tot[2] = jnp.sum(mask * divergence) * scale
    for i in range(micro):
        out_lp[i : i + 1, :] = logprob[:, i * span : (i + 1) * span]
        out_kl[i : i + 1, :] = divergence[:, i * span : (i + 1) * span]


def on_device(sizes, hidden, policy_head, reference_head, targets, loss_mask):
    vocab, section = sizes
    A, B = split_axis(vocab)
    X, C = split_axis(section)
    piece, width = hidden.shape[1], hidden.shape[2]
    devices = vocab * section
    tokens = targets.size
    gathers = (A - 1) + A * (X - 1 + B - 1) + 2 * A * (X - 1) * (B - 1)
    stats = (B * X * C - 1) + (A - 1)
    anywhere = pl.BlockSpec(memory_space=pl.ANY)
    vmem = pl.BlockSpec(memory_space=pltpu.VMEM)
    heads = policy_head.size + reference_head.size
    moments = pl.pallas_call(
        functools.partial(kernel, sizes),
        out_shape=jax.ShapeDtypeStruct((8, tokens), jnp.float32),
        in_specs=[anywhere, anywhere, anywhere, vmem],
        out_specs=vmem,
        scratch_shapes=[
            pltpu.VMEM((devices, piece, width), hidden.dtype),
            pltpu.VMEM(policy_head.shape, policy_head.dtype),
            pltpu.VMEM(reference_head.shape, reference_head.dtype),
            pltpu.VMEM((policy_head.shape[0], tokens), jnp.float32),
            pltpu.VMEM((reference_head.shape[0], tokens), jnp.float32),
            pltpu.VMEM((B * X * C, 8, tokens), jnp.float32),
            pltpu.VMEM((A, 8, tokens), jnp.float32),
            pltpu.SemaphoreType.DMA((3,)),
            pltpu.SemaphoreType.DMA((1,)),
            pltpu.SemaphoreType.DMA((PARTS,)),
            pltpu.SemaphoreType.DMA((stats,)),
            pltpu.SemaphoreType.DMA((PARTS * gathers,)),
            pltpu.SemaphoreType.DMA((stats,)),
        ],
        compiler_params=pltpu.CompilerParams(
            collective_id=0, has_side_effects=True, vmem_limit_bytes=60 * 1024 * 1024
        ),
        cost_estimate=pl.CostEstimate(
            flops=2 * tokens * heads, bytes_accessed=2 * heads, transcendentals=3 * tokens * policy_head.shape[0]
        ),
    )(hidden, policy_head, reference_head, targets)
    return pl.pallas_call(
        finish,
        out_shape=(
            jax.ShapeDtypeStruct(targets.shape, jnp.float32),
            jax.ShapeDtypeStruct(targets.shape, jnp.float32),
            jax.ShapeDtypeStruct((3,), jnp.float32),
        ),
        in_specs=[vmem, vmem],
        out_specs=(vmem, vmem, pl.BlockSpec(memory_space=pltpu.SMEM)),
    )(moments, loss_mask)


def solution(mesh):
    placed = (
        P("section", "vocab", None),
        P(("vocab", "section"), None),
        P(("vocab", "section"), None),
        P(),
        P(),
    )
    sizes = (mesh.shape["vocab"], mesh.shape["section"])
    return jax.shard_map(
        functools.partial(on_device, sizes),
        mesh=mesh, in_specs=placed, out_specs=(P(), P(), P()), check_vma=False,
    )
```

```python
import functools
import itertools

import jax
import jax.numpy as jnp
from jax import lax
from jax.experimental import pallas as pl
from jax.experimental.pallas import tpu as pltpu
from jax.sharding import PartitionSpec as P

MESH = pl.DeviceIdType.MESH


def split_axis(size):
    return (size // 2, 2) if size % 2 == 0 else (size, 1)


def power_of_two(size):
    return size & (size - 1) == 0


def flip(index, step, size):
    result = index
    bit = 1
    while bit < size:
        if step & bit:
            result = result + bit - 2 * bit * ((index // bit) % 2)
        bit *= 2
    return result


def target_of(index, step, size):
    if step == 0:
        return index
    return flip(index, step, size) if power_of_two(size) else (index + step) % size


def source_of(index, step, size):
    if step == 0:
        return index
    return flip(index, step, size) if power_of_two(size) else (index + size - step) % size


def merge(parts):
    tops = [part[0:1] for part in parts]
    rtops = [part[1:2] for part in parts]
    top = functools.reduce(jnp.maximum, tops)
    rtop = functools.reduce(jnp.maximum, rtops)
    total = first = cross = chosen = rtotal = 0.0
    for part in parts:
        shift = part[0:1] - top
        scale = jnp.exp(shift)
        total = total + scale * part[2:3]
        first = first + scale * (part[3:4] + shift * part[2:3])
        cross = cross + scale * part[4:5]
        chosen = chosen + part[5:6]
        rtotal = rtotal + jnp.exp(part[1:2] - rtop) * part[6:7]
    return top, rtop, total, first, cross, chosen, rtotal


def to_groups(values, A, B, piece):
    return jnp.concatenate(
        [
            values[m : m + 1, (i * B + j) * piece : (i * B + j + 1) * piece]
            for m in range(values.shape[0]) for j in range(B) for i in range(A)
        ],
        axis=1,
    )


def from_groups(values, micro, A, B, piece):
    starts = [((m * B + j) * A + i) * piece for m in range(micro) for i in range(A) for j in range(B)]
    return jnp.concatenate([values[:, at : at + piece] for at in starts], axis=1)


PARTS = 2
STEPS = 2


def kernel(
    sizes, hid, hp, hr, tgt, out,
    strip, rows, wp, wr, plog_acc, rlog_acc, plane, line,
    local_sem, strip_sent, strip_sem, rows_sent, core_sem, stat_sent, recv_sem, stat_sem,
):
    vocab, section = sizes
    A, B = split_axis(vocab)
    X, C = split_axis(section)
    v, s = lax.axis_index("vocab"), lax.axis_index("section")
    a, b = v // B, v % B
    x, c = s // C, s % C
    dims = (A, B, X, C)
    here = (a, b, x, c)
    piece, width = hid.shape[1], hid.shape[2]
    groups, high = rows.shape[0], rows.shape[1]
    tokens = groups * high
    count = wp.shape[0]
    share_width = width // PARTS
    step_width = share_width // STEPS
    bundle = 128 // high if tokens % 128 == 0 and 128 % high == 0 else groups
    tile = bundle * high

    def device(at):
        return (at[0] * B + at[1], at[2] * C + at[3])

    def group(at):
        return (at[2] * C + at[3]) * B + at[1]

    def to(step):
        return tuple(target_of(i, d, n) for i, d, n in zip(here, step, dims))

    def back(step):
        return tuple(source_of(i, d, n) for i, d, n in zip(here, step, dims))

    line_steps = [(d, 0, 0, 0) for d in range(1, A)]
    plane_steps = [(0,) + e for e in itertools.product(range(B), range(X), range(C)) if any(e)]
    barrier = pltpu.get_barrier_semaphore()
    for step in line_steps + plane_steps:
        pl.semaphore_signal(barrier, inc=1, device_id=device(to(step)), device_id_type=MESH)

    own = pltpu.make_async_copy(hid.at[0], strip.at[a], local_sem.at[0])
    own.start()
    load_p = pltpu.make_async_copy(hp, wp, local_sem.at[1])
    load_p.start()
    load_r = pltpu.make_async_copy(hr, wr, local_sem.at[2])
    load_r.start()
    plog_acc[...] = jnp.zeros_like(plog_acc)
    rlog_acc[...] = jnp.zeros_like(rlog_acc)
    wanted = to_groups(tgt[...], A, B, piece)
    own.wait()
    pl.semaphore_wait(barrier, len(line_steps) + len(plane_steps))

    keys = {}

    def view(at, h, half):
        lo, size = h * share_width, share_width
        if half is not None:
            size = share_width // 2
            lo = lo + half * size
        return rows.at[group(at), :, pl.ds(lo, size)]

    def describe(key, step, at, h, half):
        part = view(at, h, half)
        if key[0] == "core":
            arrived = core_sem.at[h]
        else:
            arrived = recv_sem.at[keys.setdefault((h,) + key, len(keys))]
        return pltpu.make_async_remote_copy(
            src_ref=part, dst_ref=part, send_sem=rows_sent.at[0], recv_sem=arrived,
            device_id=device(to(step)), device_id_type=MESH,
        )

    def copy(key, step, at, h, half=None):
        describe(key, step, at, h, half).start()

    def arrive(key, step, at, h, half=None):
        describe(key, step, at, h, half).wait_recv()

    def to_cores(step, h):
        for dc in range(1, C):
            copy(("core", step, dc), (0, 0, 0, dc), back(step), h)

    def send_strip(h):
        part = strip.at[a, :, pl.ds(h * share_width, share_width)]
        for step in line_steps:
            pltpu.make_async_remote_copy(
                src_ref=part, dst_ref=part, send_sem=strip_sent.at[0], recv_sem=strip_sem.at[h],
                device_id=device(to(step)), device_id_type=MESH,
            ).start()

    def fan(h):
        columns = pl.ds(h * share_width, share_width)
        if A > 1:
            part = strip.at[pl.ds(0, A - 1), :, columns]
            pltpu.make_async_copy(part, part, strip_sem.at[h]).wait()
        rows[group(here), :, columns] = jnp.concatenate(
            [strip[i, :, columns] for i in range(A)], axis=0
        )
        for dx in range(1, X):
            copy(("x", dx), (0, 0, dx, 0), here, h)
        for db in range(1, B):
            copy(("b", db), (0, db, 0, 0), here, h)
        to_cores((0, 0, 0, 0), h)

    def cross(h):
        for dx in range(1, X):
            at = back((0, 0, dx, 0))
            arrive(("x", dx), (0, 0, dx, 0), at, h)
            for db in range(1, B):
                copy(("xb", dx, db), (0, db, 0, 0), at, h, 0)
        for db in range(1, B):
            at = back((0, db, 0, 0))
            arrive(("b", db), (0, db, 0, 0), at, h)
            for dx in range(1, X):
                copy(("bx", dx, db), (0, 0, dx, 0), at, h, 1)
        for dx in range(1, X):
            to_cores((0, 0, dx, 0), h)
        for db in range(1, B):
            to_cores((0, db, 0, 0), h)

    def corner(h):
        for dx in range(1, X):
            for db in range(1, B):
                at = back((0, db, dx, 0))
                arrive(("xb", dx, db), (0, db, 0, 0), at, h, 0)
                arrive(("bx", dx, db), (0, 0, dx, 0), at, h, 1)
                to_cores((0, db, dx, 0), h)

    def from_cores(h):
        if C > 1:
            part = rows.at[pl.ds(0, groups // C * (C - 1)), :, pl.ds(0, share_width)]
            pltpu.make_async_copy(part, part, core_sem.at[h]).wait()

    dims_nt = (((1,), (1,)), ((), ()))

    def multiply(k):
        columns = pl.ds(k * step_width, step_width)

        def tile_of(n):
            mine = rows[pl.ds(n * bundle, bundle), :, columns].reshape(tile, step_width)
            place = pl.ds(n * tile if isinstance(n, int) else pl.multiple_of(n * tile, tile), tile)
            plog_acc[:, place] += lax.dot_general(
                wp[:, columns], mine, dims_nt, preferred_element_type=jnp.float32
            )
            rlog_acc[:, place] += lax.dot_general(
                wr[:, columns], mine, dims_nt, preferred_element_type=jnp.float32
            )

        if tokens == tile:
            tile_of(0)
        else:
            pl.loop(0, tokens // tile)(tile_of)

    for h in range(PARTS):
        send_strip(h)
    for u in range(PARTS + 1):
        if u < PARTS:
            fan(u)
        if 1 <= u:
            cross(u - 1)
        if 2 <= u:
            corner(u - 2)
    load_p.wait()
    load_r.wait()
    early = (PARTS - 1) * STEPS
    for k in range(early):
        if k % STEPS == 0:
            from_cores(k // STEPS)
        if k == early // 2:
            corner(PARTS - 1)
        multiply(k)
    if not early:
        corner(PARTS - 1)
    from_cores(PARTS - 1)
    for k in range(early, PARTS * STEPS):
        multiply(k)

    offset = (v * section + s) * count
    moments = []
    for n in range(tokens // tile):
        place = slice(n * tile, (n + 1) * tile)
        plog, rlog = plog_acc[:, place], rlog_acc[:, place]
        top = jnp.max(plog, axis=0, keepdims=True)
        shift = plog - top
        weight = jnp.exp(shift)
        total = jnp.sum(weight, axis=0, keepdims=True)
        first = jnp.sum(weight * shift, axis=0, keepdims=True)
        across = jnp.sum(weight * (plog - rlog), axis=0, keepdims=True)
        ids = offset + lax.broadcasted_iota(jnp.int32, plog.shape, 0)
        chosen = jnp.sum(jnp.where(ids == wanted[:, place], plog, 0.0), axis=0, keepdims=True)
        rtop = jnp.max(rlog, axis=0, keepdims=True)
        rtotal = jnp.sum(jnp.exp(rlog - rtop), axis=0, keepdims=True)
        moments.append(
            jnp.concatenate([top, rtop, total, first, across, chosen, rtotal, jnp.zeros_like(top)], axis=0)
        )
    index = b * (X * C) + x * C + c
    plane[index] = jnp.concatenate(moments, axis=1) if len(moments) > 1 else moments[0]

    shared = []

    def share(step, buffer, at, start):
        i = keys.setdefault(("stat", step), len(keys)) - gather_keys
        op = pltpu.make_async_remote_copy(
            src_ref=buffer.at[at], dst_ref=buffer.at[at],
            send_sem=stat_sent.at[i], recv_sem=stat_sem.at[i],
            device_id=device(to(step)), device_id_type=MESH,
        )
        if start:
            op.start()
            shared.append(op)
        else:
            op.wait_recv()

    def plane_index(at):
        return at[1] * (X * C) + at[2] * C + at[3]

    gather_keys = len(keys)
    for step in plane_steps:
        share(step, plane, plane_index(here), True)
    if A > 1:
        sent = strip.at[pl.ds(0, A - 1)]
        pltpu.make_async_copy(sent, sent, strip_sent.at[0]).wait()
    if groups > 1:
        sent = rows.at[pl.ds(0, groups - 1)]
        pltpu.make_async_copy(sent, sent, rows_sent.at[0]).wait()
    for step in plane_steps:
        share(step, plane, plane_index(back(step)), False)
    merged = merge([plane[i] for i in range(B * X * C)])
    line[a] = jnp.concatenate(list(merged) + [jnp.zeros_like(merged[0])], axis=0)
    for step in line_steps:
        share(step, line, a, True)
    for step in line_steps:
        share(step, line, back(step)[0], False)
    merged = merge([line[i] for i in range(A)])
    out[...] = jnp.concatenate(list(merged) + [jnp.zeros_like(merged[0])], axis=0)
    for op in shared:
        op.wait_send()


def finish(A, B, stats, msk, out_lp, out_kl, out_tot):
    micro, span = msk.shape
    ordered = from_groups(stats[...], micro, A, B, span // (A * B))
    top, rtop, total, first, across, chosen, rtotal = [ordered[i : i + 1, :] for i in range(7)]
    log_total = jnp.log(total)
    lse = top + log_total
    logprob = chosen - lse
    entropy = log_total - first / total
    divergence = across / total - lse + (rtop + jnp.log(rtotal))
    mask = jnp.concatenate([msk[i : i + 1, :] for i in range(micro)], axis=1).astype(jnp.float32)
    scale = 1.0 / (micro * span)
    out_tot[0] = jnp.sum(mask * logprob) * scale
    out_tot[1] = jnp.sum(mask * entropy) * scale
    out_tot[2] = jnp.sum(mask * divergence) * scale
    for i in range(micro):
        out_lp[i : i + 1, :] = logprob[:, i * span : (i + 1) * span]
        out_kl[i : i + 1, :] = divergence[:, i * span : (i + 1) * span]


def on_device(sizes, hidden, policy_head, reference_head, targets, loss_mask):
    vocab, section = sizes
    A, B = split_axis(vocab)
    X, C = split_axis(section)
    piece, width = hidden.shape[1], hidden.shape[2]
    tokens = targets.size
    gathers = (X - 1) + (B - 1) + 2 * (X - 1) * (B - 1)
    stats = (B * X * C - 1) + (A - 1)
    anywhere = pl.BlockSpec(memory_space=pl.ANY)
    vmem = pl.BlockSpec(memory_space=pltpu.VMEM)
    heads = policy_head.size + reference_head.size
    moments = pl.pallas_call(
        functools.partial(kernel, sizes),
        out_shape=jax.ShapeDtypeStruct((8, tokens), jnp.float32),
        in_specs=[anywhere, anywhere, anywhere, vmem],
        out_specs=vmem,
        scratch_shapes=[
            pltpu.VMEM((A, piece, width), hidden.dtype),
            pltpu.VMEM((B * X * C, A * piece, width), hidden.dtype),
            pltpu.VMEM(policy_head.shape, policy_head.dtype),
            pltpu.VMEM(reference_head.shape, reference_head.dtype),
            pltpu.VMEM((policy_head.shape[0], tokens), jnp.float32),
            pltpu.VMEM((reference_head.shape[0], tokens), jnp.float32),
            pltpu.VMEM((B * X * C, 8, tokens), jnp.float32),
            pltpu.VMEM((A, 8, tokens), jnp.float32),
            pltpu.SemaphoreType.DMA((3,)),
            pltpu.SemaphoreType.DMA((1,)),
            pltpu.SemaphoreType.DMA((PARTS,)),
            pltpu.SemaphoreType.DMA((1,)),
            pltpu.SemaphoreType.DMA((PARTS,)),
            pltpu.SemaphoreType.DMA((stats,)),
            pltpu.SemaphoreType.DMA((PARTS * gathers,)),
            pltpu.SemaphoreType.DMA((stats,)),
        ],
        compiler_params=pltpu.CompilerParams(
            collective_id=0, has_side_effects=True, vmem_limit_bytes=60 * 1024 * 1024
        ),
        cost_estimate=pl.CostEstimate(
            flops=2 * tokens * heads, bytes_accessed=2 * heads, transcendentals=3 * tokens * policy_head.shape[0]
        ),
    )(hidden, policy_head, reference_head, targets)
    return pl.pallas_call(
        functools.partial(finish, A, B),
        out_shape=(
            jax.ShapeDtypeStruct(targets.shape, jnp.float32),
            jax.ShapeDtypeStruct(targets.shape, jnp.float32),
            jax.ShapeDtypeStruct((3,), jnp.float32),
        ),
        in_specs=[vmem, vmem],
        out_specs=(vmem, vmem, pl.BlockSpec(memory_space=pltpu.SMEM)),
    )(moments, loss_mask)


def solution(mesh):
    placed = (
        P("section", "vocab", None),
        P(("vocab", "section"), None),
        P(("vocab", "section"), None),
        P(),
        P(),
    )
    sizes = (mesh.shape["vocab"], mesh.shape["section"])
    return jax.shard_map(
        functools.partial(on_device, sizes),
        mesh=mesh, in_specs=placed, out_specs=(P(), P(), P()), check_vma=False,
    )
```

```python
import functools
import itertools

import jax
import jax.numpy as jnp
from jax import lax
from jax.experimental import pallas as pl
from jax.experimental.pallas import tpu as pltpu
from jax.sharding import PartitionSpec as P

MESH = pl.DeviceIdType.MESH


def split_axis(size):
    return (size // 2, 2) if size % 2 == 0 else (size, 1)


def power_of_two(size):
    return size & (size - 1) == 0


def flip(index, step, size):
    result = index
    bit = 1
    while bit < size:
        if step & bit:
            result = result + bit - 2 * bit * ((index // bit) % 2)
        bit *= 2
    return result


def target_of(index, step, size):
    if step == 0:
        return index
    return flip(index, step, size) if power_of_two(size) else (index + step) % size


def source_of(index, step, size):
    if step == 0:
        return index
    return flip(index, step, size) if power_of_two(size) else (index + size - step) % size


def merge(parts):
    top = functools.reduce(jnp.maximum, [part[8:16] for part in parts])
    total = sum(jnp.exp(part[8:16] - top) * part[0:8] for part in parts)
    return total, top


def to_groups(values, A, B, piece):
    return jnp.concatenate(
        [
            values[m : m + 1, (i * B + j) * piece : (i * B + j + 1) * piece]
            for m in range(values.shape[0]) for j in range(B) for i in range(A)
        ],
        axis=1,
    )


def from_groups(values, micro, A, B, piece):
    starts = [((m * B + j) * A + i) * piece for m in range(micro) for i in range(A) for j in range(B)]
    return jnp.concatenate([values[:, at : at + piece] for at in starts], axis=1)


PARTS = 2
STEPS = 2


def kernel(
    sizes, hid, hp, hr, tgt, out,
    strip, rows, wp, wr, acc, plane, line,
    local_sem, strip_sent, strip_sem, rows_sent, core_sem, recv_sem, stat_sent, stat_sem,
):
    vocab, section = sizes
    A, B = split_axis(vocab)
    X, C = split_axis(section)
    v, s = lax.axis_index("vocab"), lax.axis_index("section")
    a, b = v // B, v % B
    x, c = s // C, s % C
    dims = (A, B, X, C)
    here = (a, b, x, c)
    piece, width = hid.shape[1], hid.shape[2]
    groups, high = rows.shape[0], rows.shape[1]
    tokens = groups * high
    count = wp.shape[0]
    whole = acc.shape[0] - count
    share_width = width // PARTS
    step_width = share_width // STEPS
    bundle = 128 // high if tokens % 128 == 0 and 128 % high == 0 else groups
    tile = bundle * high

    def device(at):
        return (at[0] * B + at[1], at[2] * C + at[3])

    def group(at):
        return (at[2] * C + at[3]) * B + at[1]

    def to(step):
        return tuple(target_of(i, d, n) for i, d, n in zip(here, step, dims))

    def back(step):
        return tuple(source_of(i, d, n) for i, d, n in zip(here, step, dims))

    line_steps = [(d, 0, 0, 0) for d in range(1, A)]
    plane_steps = [(0,) + e for e in itertools.product(range(B), range(X), range(C)) if any(e)]
    barrier = pltpu.get_barrier_semaphore()
    for step in line_steps + plane_steps:
        pl.semaphore_signal(barrier, inc=1, device_id=device(to(step)), device_id_type=MESH)

    own = pltpu.make_async_copy(hid.at[0], strip.at[a], local_sem.at[0])
    own.start()
    wanted = to_groups(tgt[...], A, B, piece)
    own.wait()
    pl.semaphore_wait(barrier, len(line_steps) + len(plane_steps))

    keys = {}

    def view(at, h, half):
        lo, size = h * share_width, share_width
        if half is not None:
            size = share_width // 2
            lo = lo + half * size
        return rows.at[group(at), :, pl.ds(lo, size)]

    def describe(key, step, at, h, half):
        part = view(at, h, half)
        if key[0] == "core":
            arrived = core_sem.at[h]
        else:
            arrived = recv_sem.at[keys.setdefault((h,) + key, len(keys))]
        return pltpu.make_async_remote_copy(
            src_ref=part, dst_ref=part, send_sem=rows_sent.at[0], recv_sem=arrived,
            device_id=device(to(step)), device_id_type=MESH,
        )

    def copy(key, step, at, h, half=None):
        describe(key, step, at, h, half).start()

    def arrive(key, step, at, h, half=None):
        describe(key, step, at, h, half).wait_recv()

    def to_cores(step, h):
        for dc in range(1, C):
            copy(("core", step, dc), (0, 0, 0, dc), back(step), h)

    def send_strip(h):
        part = strip.at[a, :, pl.ds(h * share_width, share_width)]
        for step in line_steps:
            pltpu.make_async_remote_copy(
                src_ref=part, dst_ref=part, send_sem=strip_sent.at[0], recv_sem=strip_sem.at[h],
                device_id=device(to(step)), device_id_type=MESH,
            ).start()

    def fan(h):
        columns = pl.ds(h * share_width, share_width)
        if A > 1:
            part = strip.at[pl.ds(0, A - 1), :, columns]
            pltpu.make_async_copy(part, part, strip_sem.at[h]).wait()
        rows[group(here), :, columns] = jnp.concatenate(
            [strip[i, :, columns] for i in range(A)], axis=0
        )
        for dx in range(1, X):
            copy(("x", dx), (0, 0, dx, 0), here, h)
        for db in range(1, B):
            copy(("b", db), (0, db, 0, 0), here, h)
        to_cores((0, 0, 0, 0), h)

    def cross(h):
        for dx in range(1, X):
            at = back((0, 0, dx, 0))
            arrive(("x", dx), (0, 0, dx, 0), at, h)
            for db in range(1, B):
                copy(("xb", dx, db), (0, db, 0, 0), at, h, 0)
        for db in range(1, B):
            at = back((0, db, 0, 0))
            arrive(("b", db), (0, db, 0, 0), at, h)
            for dx in range(1, X):
                copy(("bx", dx, db), (0, 0, dx, 0), at, h, 1)
        for dx in range(1, X):
            to_cores((0, 0, dx, 0), h)
        for db in range(1, B):
            to_cores((0, db, 0, 0), h)

    def corner(h):
        for dx in range(1, X):
            for db in range(1, B):
                at = back((0, db, dx, 0))
                arrive(("xb", dx, db), (0, db, 0, 0), at, h, 0)
                arrive(("bx", dx, db), (0, 0, dx, 0), at, h, 1)
                to_cores((0, db, dx, 0), h)

    def from_cores(h):
        if C > 1:
            part = rows.at[pl.ds(0, groups // C * (C - 1)), :, pl.ds(0, share_width)]
            pltpu.make_async_copy(part, part, core_sem.at[h]).wait()

    dims_nt = (((1,), (1,)), ((), ()))

    def multiply(k):
        columns = pl.ds(k * step_width, step_width)

        def tile_of(n):
            mine = rows[pl.ds(n * bundle, bundle), :, columns].reshape(tile, step_width)
            place = pl.ds(n * tile if isinstance(n, int) else pl.multiple_of(n * tile, tile), tile)
            heads = jnp.concatenate(
                [wp[:, columns], jnp.zeros((whole - count, step_width), wp.dtype), wr[:, columns]], axis=0
            )
            logits = lax.dot_general(heads, mine, dims_nt, preferred_element_type=jnp.float32)
            if k == 0:
                acc[:, place] = logits
            else:
                acc[:, place] += logits

        if tokens == tile:
            tile_of(0)
        else:
            pl.loop(0, tokens // tile)(tile_of)

    for h in range(PARTS):
        send_strip(h)
    load_p = pltpu.make_async_copy(hp, wp, local_sem.at[1])
    load_p.start()
    load_r = pltpu.make_async_copy(hr, wr, local_sem.at[2])
    load_r.start()
    for u in range(PARTS + 1):
        if u < PARTS:
            fan(u)
        if 1 <= u:
            cross(u - 1)
        if 2 <= u:
            corner(u - 2)
    load_p.wait()
    load_r.wait()
    early = (PARTS - 1) * STEPS
    for k in range(early):
        if k % STEPS == 0:
            from_cores(k // STEPS)
        if k == early // 2:
            corner(PARTS - 1)
        multiply(k)
    if not early:
        corner(PARTS - 1)
    from_cores(PARTS - 1)
    for k in range(early, PARTS * STEPS):
        multiply(k)

    offset = (v * section + s) * count
    moments = []
    for n in range(tokens // tile):
        place = slice(n * tile, (n + 1) * tile)
        plog, rlog = acc[0:count, place], acc[whole : whole + count, place]
        top = jnp.max(plog, axis=0, keepdims=True)
        shift = plog - top
        weight = jnp.exp(shift)
        total = jnp.sum(weight, axis=0, keepdims=True)
        first = jnp.sum(weight * plog, axis=0, keepdims=True)
        across = jnp.sum(weight * (plog - rlog), axis=0, keepdims=True)
        ids = offset + lax.broadcasted_iota(jnp.int32, plog.shape, 0)
        chosen = jnp.sum(jnp.where(ids == wanted[:, place], plog, 0.0), axis=0, keepdims=True)
        rtop = jnp.max(rlog, axis=0, keepdims=True)
        rtotal = jnp.sum(jnp.exp(rlog - rtop), axis=0, keepdims=True)
        none = jnp.zeros_like(top)
        moments.append(
            jnp.concatenate(
                [total, first, across, rtotal, chosen, none, none, none]
                + [top, top, top, rtop, none, none, none, none],
                axis=0,
            )
        )
    index = b * (X * C) + x * C + c
    plane[index] = jnp.concatenate(moments, axis=1) if len(moments) > 1 else moments[0]

    def exchange(i, steps, buffer, position):
        part = buffer.at[position]
        for step in steps:
            pltpu.make_async_remote_copy(
                src_ref=part, dst_ref=part, send_sem=stat_sent.at[i], recv_sem=stat_sem.at[i],
                device_id=device(to(step)), device_id_type=MESH,
            ).start()

    def exchanged(i, steps, buffer, sem):
        if steps:
            part = buffer.at[pl.ds(0, len(steps))]
            pltpu.make_async_copy(part, part, sem.at[i]).wait()

    exchange(0, plane_steps, plane, index)
    if A > 1:
        sent = strip.at[pl.ds(0, A - 1)]
        pltpu.make_async_copy(sent, sent, strip_sent.at[0]).wait()
    if groups > 1:
        sent = rows.at[pl.ds(0, groups - 1)]
        pltpu.make_async_copy(sent, sent, rows_sent.at[0]).wait()
    exchanged(0, plane_steps, plane, stat_sem)
    line[a] = jnp.concatenate(merge([plane[i] for i in range(B * X * C)]), axis=0)
    exchange(1, line_steps, line, a)
    exchanged(0, plane_steps, plane, stat_sent)
    exchanged(1, line_steps, line, stat_sem)
    total, top = merge([line[i] for i in range(A)])
    out[...] = jnp.concatenate([total[0:5], top[0:1], top[3:4], total[7:8]], axis=0)
    exchanged(1, line_steps, line, stat_sent)


def finish(A, B, stats, msk, out_lp, out_kl, out_tot):
    micro, span = msk.shape
    ordered = from_groups(stats[...], micro, A, B, span // (A * B))
    total, first, across, rtotal, chosen, top, rtop = [ordered[i : i + 1, :] for i in range(7)]
    lse = top + jnp.log(total)
    logprob = chosen - lse
    entropy = lse - first / total
    divergence = across / total - lse + (rtop + jnp.log(rtotal))
    mask = jnp.concatenate([msk[i : i + 1, :] for i in range(micro)], axis=1).astype(jnp.float32)
    scale = 1.0 / (micro * span)
    out_tot[0] = jnp.sum(mask * logprob) * scale
    out_tot[1] = jnp.sum(mask * entropy) * scale
    out_tot[2] = jnp.sum(mask * divergence) * scale
    for i in range(micro):
        out_lp[i : i + 1, :] = logprob[:, i * span : (i + 1) * span]
        out_kl[i : i + 1, :] = divergence[:, i * span : (i + 1) * span]


def on_device(sizes, hidden, policy_head, reference_head, targets, loss_mask):
    vocab, section = sizes
    A, B = split_axis(vocab)
    X, C = split_axis(section)
    piece, width = hidden.shape[1], hidden.shape[2]
    tokens = targets.size
    gathers = (X - 1) + (B - 1) + 2 * (X - 1) * (B - 1)
    anywhere = pl.BlockSpec(memory_space=pl.ANY)
    vmem = pl.BlockSpec(memory_space=pltpu.VMEM)
    heads = policy_head.size + reference_head.size
    moments = pl.pallas_call(
        functools.partial(kernel, sizes),
        out_shape=jax.ShapeDtypeStruct((8, tokens), jnp.float32),
        in_specs=[anywhere, anywhere, anywhere, vmem],
        out_specs=vmem,
        scratch_shapes=[
            pltpu.VMEM((A, piece, width), hidden.dtype),
            pltpu.VMEM((B * X * C, A * piece, width), hidden.dtype),
            pltpu.VMEM(policy_head.shape, policy_head.dtype),
            pltpu.VMEM(reference_head.shape, reference_head.dtype),
            pltpu.VMEM((-(-policy_head.shape[0] // 16) * 16 + reference_head.shape[0], tokens), jnp.float32),
            pltpu.VMEM((B * X * C, 16, tokens), jnp.float32),
            pltpu.VMEM((A, 16, tokens), jnp.float32),
            pltpu.SemaphoreType.DMA((3,)),
            pltpu.SemaphoreType.DMA((1,)),
            pltpu.SemaphoreType.DMA((PARTS,)),
            pltpu.SemaphoreType.DMA((1,)),
            pltpu.SemaphoreType.DMA((PARTS,)),
            pltpu.SemaphoreType.DMA((PARTS * gathers,)),
            pltpu.SemaphoreType.DMA((2,)),
            pltpu.SemaphoreType.DMA((2,)),
        ],
        compiler_params=pltpu.CompilerParams(
            collective_id=0, has_side_effects=True, vmem_limit_bytes=60 * 1024 * 1024
        ),
        cost_estimate=pl.CostEstimate(
            flops=2 * tokens * heads, bytes_accessed=2 * heads, transcendentals=3 * tokens * policy_head.shape[0]
        ),
    )(hidden, policy_head, reference_head, targets)
    return pl.pallas_call(
        functools.partial(finish, A, B),
        out_shape=(
            jax.ShapeDtypeStruct(targets.shape, jnp.float32),
            jax.ShapeDtypeStruct(targets.shape, jnp.float32),
            jax.ShapeDtypeStruct((3,), jnp.float32),
        ),
        in_specs=[vmem, vmem],
        out_specs=(vmem, vmem, pl.BlockSpec(memory_space=pltpu.SMEM)),
    )(moments, loss_mask)


def solution(mesh):
    placed = (
        P("section", "vocab", None),
        P(("vocab", "section"), None),
        P(("vocab", "section"), None),
        P(),
        P(),
    )
    sizes = (mesh.shape["vocab"], mesh.shape["section"])
    return jax.shard_map(
        functools.partial(on_device, sizes),
        mesh=mesh, in_specs=placed, out_specs=(P(), P(), P()), check_vma=False,
    )
```

```python
import functools
import itertools

import jax
import jax.numpy as jnp
from jax import lax
from jax.experimental import pallas as pl
from jax.experimental.pallas import tpu as pltpu
from jax.sharding import PartitionSpec as P

MESH = pl.DeviceIdType.MESH


def split_axis(size):
    return (size // 2, 2) if size % 2 == 0 else (size, 1)


def power_of_two(size):
    return size & (size - 1) == 0


def flip(index, step, size):
    result = index
    bit = 1
    while bit < size:
        if step & bit:
            result = result + bit - 2 * bit * ((index // bit) % 2)
        bit *= 2
    return result


def target_of(index, step, size):
    if step == 0:
        return index
    return flip(index, step, size) if power_of_two(size) else (index + step) % size


def source_of(index, step, size):
    if step == 0:
        return index
    return flip(index, step, size) if power_of_two(size) else (index + size - step) % size


def merge(parts):
    top = functools.reduce(jnp.maximum, [part[8:16] for part in parts])
    total = sum(jnp.exp(part[8:16] - top) * part[0:8] for part in parts)
    return total, top


def to_groups(values, A, B, piece):
    return jnp.concatenate(
        [
            values[m : m + 1, (i * B + j) * piece : (i * B + j + 1) * piece]
            for m in range(values.shape[0]) for j in range(B) for i in range(A)
        ],
        axis=1,
    )


def from_groups(values, micro, A, B, piece):
    starts = [((m * B + j) * A + i) * piece for m in range(micro) for i in range(A) for j in range(B)]
    return jnp.concatenate([values[:, at : at + piece] for at in starts], axis=1)


PARTS = 2
STEPS = 2


def kernel(
    sizes, hid, hp, hr, tgt, out,
    strip, rows, wp, wr, plog_acc, rlog_acc, plane, line,
    local_sem, strip_sent, strip_sem, rows_sent, core_sem, recv_sem, stat_sent, stat_sem,
):
    vocab, section = sizes
    A, B = split_axis(vocab)
    X, C = split_axis(section)
    v, s = lax.axis_index("vocab"), lax.axis_index("section")
    a, b = v // B, v % B
    x, c = s // C, s % C
    dims = (A, B, X, C)
    here = (a, b, x, c)
    piece, width = hid.shape[1], hid.shape[2]
    groups, high = rows.shape[0], rows.shape[1]
    tokens = groups * high
    count = wp.shape[0]
    share_width = width // PARTS
    step_width = share_width // STEPS
    bundle = 128 // high if tokens % 128 == 0 and 128 % high == 0 else groups
    tile = bundle * high

    def device(at):
        return (at[0] * B + at[1], at[2] * C + at[3])

    def group(at):
        return (at[2] * C + at[3]) * B + at[1]

    def to(step):
        return tuple(target_of(i, d, n) for i, d, n in zip(here, step, dims))

    def back(step):
        return tuple(source_of(i, d, n) for i, d, n in zip(here, step, dims))

    line_steps = [(d, 0, 0, 0) for d in range(1, A)]
    plane_steps = [(0,) + e for e in itertools.product(range(B), range(X), range(C)) if any(e)]
    barrier = pltpu.get_barrier_semaphore()
    for step in line_steps + plane_steps:
        pl.semaphore_signal(barrier, inc=1, device_id=device(to(step)), device_id_type=MESH)

    own = pltpu.make_async_copy(hid.at[0], strip.at[a], local_sem.at[0])
    own.start()
    load_p = pltpu.make_async_copy(hp, wp, local_sem.at[1])
    load_p.start()
    load_r = pltpu.make_async_copy(hr, wr, local_sem.at[2])
    load_r.start()
    wanted = to_groups(tgt[...], A, B, piece)
    own.wait()
    pl.semaphore_wait(barrier, len(line_steps) + len(plane_steps))

    keys = {}

    def view(at, h, half):
        lo, size = h * share_width, share_width
        if half is not None:
            size = share_width // 2
            lo = lo + half * size
        return rows.at[group(at), :, pl.ds(lo, size)]

    def describe(key, step, at, h, half):
        part = view(at, h, half)
        if key[0] == "core":
            arrived = core_sem.at[h]
        else:
            arrived = recv_sem.at[keys.setdefault((h,) + key, len(keys))]
        return pltpu.make_async_remote_copy(
            src_ref=part, dst_ref=part, send_sem=rows_sent.at[0], recv_sem=arrived,
            device_id=device(to(step)), device_id_type=MESH,
        )

    def copy(key, step, at, h, half=None):
        describe(key, step, at, h, half).start()

    def arrive(key, step, at, h, half=None):
        describe(key, step, at, h, half).wait_recv()

    def to_cores(step, h):
        for dc in range(1, C):
            copy(("core", step, dc), (0, 0, 0, dc), back(step), h)

    def send_strip(h):
        part = strip.at[a, :, pl.ds(h * share_width, share_width)]
        for step in line_steps:
            pltpu.make_async_remote_copy(
                src_ref=part, dst_ref=part, send_sem=strip_sent.at[0], recv_sem=strip_sem.at[h],
                device_id=device(to(step)), device_id_type=MESH,
            ).start()

    def fan(h):
        columns = pl.ds(h * share_width, share_width)
        if A > 1:
            part = strip.at[pl.ds(0, A - 1), :, columns]
            pltpu.make_async_copy(part, part, strip_sem.at[h]).wait()
        rows[group(here), :, columns] = jnp.concatenate(
            [strip[i, :, columns] for i in range(A)], axis=0
        )
        for dx in range(1, X):
            copy(("x", dx), (0, 0, dx, 0), here, h)
        for db in range(1, B):
            copy(("b", db), (0, db, 0, 0), here, h)
        to_cores((0, 0, 0, 0), h)

    def cross(h):
        for dx in range(1, X):
            at = back((0, 0, dx, 0))
            arrive(("x", dx), (0, 0, dx, 0), at, h)
            for db in range(1, B):
                copy(("xb", dx, db), (0, db, 0, 0), at, h, 0)
        for db in range(1, B):
            at = back((0, db, 0, 0))
            arrive(("b", db), (0, db, 0, 0), at, h)
            for dx in range(1, X):
                copy(("bx", dx, db), (0, 0, dx, 0), at, h, 1)
        for dx in range(1, X):
            to_cores((0, 0, dx, 0), h)
        for db in range(1, B):
            to_cores((0, db, 0, 0), h)

    def corner(h):
        for dx in range(1, X):
            for db in range(1, B):
                at = back((0, db, dx, 0))
                arrive(("xb", dx, db), (0, db, 0, 0), at, h, 0)
                arrive(("bx", dx, db), (0, 0, dx, 0), at, h, 1)
                to_cores((0, db, dx, 0), h)

    def from_cores(h):
        if C > 1:
            part = rows.at[pl.ds(0, groups // C * (C - 1)), :, pl.ds(0, share_width)]
            pltpu.make_async_copy(part, part, core_sem.at[h]).wait()

    dims_nt = (((1,), (1,)), ((), ()))

    def multiply(k):
        columns = pl.ds(k * step_width, step_width)

        def tile_of(n):
            mine = rows[pl.ds(n * bundle, bundle), :, columns].reshape(tile, step_width)
            place = pl.ds(n * tile if isinstance(n, int) else pl.multiple_of(n * tile, tile), tile)
            for head, total in ((wp, plog_acc), (wr, rlog_acc)):
                logits = lax.dot_general(
                    head[:, columns], mine, dims_nt, preferred_element_type=jnp.float32
                )
                if k == 0:
                    total[:, place] = logits
                else:
                    total[:, place] += logits

        if tokens == tile:
            tile_of(0)
        else:
            pl.loop(0, tokens // tile)(tile_of)

    for h in range(PARTS):
        send_strip(h)
    for u in range(PARTS + 1):
        if u < PARTS:
            fan(u)
        if 1 <= u:
            cross(u - 1)
        if 2 <= u:
            corner(u - 2)
    load_p.wait()
    load_r.wait()
    corner(PARTS - 1)
    for k in range(PARTS * STEPS):
        if k % STEPS == 0:
            from_cores(k // STEPS)
        multiply(k)

    offset = (v * section + s) * count
    moments = []
    for n in range(tokens // tile):
        place = slice(n * tile, (n + 1) * tile)
        plog, rlog = plog_acc[:, place], rlog_acc[:, place]
        top = jnp.max(plog, axis=0, keepdims=True)
        shift = plog - top
        weight = jnp.exp(shift)
        total = jnp.sum(weight, axis=0, keepdims=True)
        first = jnp.sum(weight * plog, axis=0, keepdims=True)
        across = jnp.sum(weight * (plog - rlog), axis=0, keepdims=True)
        ids = offset + lax.broadcasted_iota(jnp.int32, plog.shape, 0)
        chosen = jnp.sum(jnp.where(ids == wanted[:, place], plog, 0.0), axis=0, keepdims=True)
        rtop = jnp.max(rlog, axis=0, keepdims=True)
        rtotal = jnp.sum(jnp.exp(rlog - rtop), axis=0, keepdims=True)
        none = jnp.zeros_like(top)
        moments.append(
            jnp.concatenate(
                [total, first, across, rtotal, chosen, none, none, none]
                + [top, top, top, rtop, none, none, none, none],
                axis=0,
            )
        )
    index = b * (X * C) + x * C + c
    plane[index] = jnp.concatenate(moments, axis=1) if len(moments) > 1 else moments[0]

    def exchange(i, steps, buffer, position):
        part = buffer.at[position]
        for step in steps:
            pltpu.make_async_remote_copy(
                src_ref=part, dst_ref=part, send_sem=stat_sent.at[i], recv_sem=stat_sem.at[i],
                device_id=device(to(step)), device_id_type=MESH,
            ).start()

    def exchanged(i, steps, buffer, sem):
        if steps:
            part = buffer.at[pl.ds(0, len(steps))]
            pltpu.make_async_copy(part, part, sem.at[i]).wait()

    exchange(0, plane_steps, plane, index)
    if A > 1:
        sent = strip.at[pl.ds(0, A - 1)]
        pltpu.make_async_copy(sent, sent, strip_sent.at[0]).wait()
    if groups > 1:
        sent = rows.at[pl.ds(0, groups - 1)]
        pltpu.make_async_copy(sent, sent, rows_sent.at[0]).wait()
    exchanged(0, plane_steps, plane, stat_sem)
    line[a] = jnp.concatenate(merge([plane[i] for i in range(B * X * C)]), axis=0)
    exchange(1, line_steps, line, a)
    exchanged(0, plane_steps, plane, stat_sent)
    exchanged(1, line_steps, line, stat_sem)
    total, top = merge([line[i] for i in range(A)])
    out[...] = jnp.concatenate([total[0:5], top[0:1], top[3:4], total[7:8]], axis=0)
    exchanged(1, line_steps, line, stat_sent)


def finish(A, B, stats, msk, out_lp, out_kl, out_tot):
    micro, span = msk.shape
    ordered = from_groups(stats[...], micro, A, B, span // (A * B))
    total, first, across, rtotal, chosen, top, rtop = [ordered[i : i + 1, :] for i in range(7)]
    lse = top + jnp.log(total)
    logprob = chosen - lse
    entropy = lse - first / total
    divergence = across / total - lse + (rtop + jnp.log(rtotal))
    mask = jnp.concatenate([msk[i : i + 1, :] for i in range(micro)], axis=1).astype(jnp.float32)
    scale = 1.0 / (micro * span)
    out_tot[0] = jnp.sum(mask * logprob) * scale
    out_tot[1] = jnp.sum(mask * entropy) * scale
    out_tot[2] = jnp.sum(mask * divergence) * scale
    for i in range(micro):
        out_lp[i : i + 1, :] = logprob[:, i * span : (i + 1) * span]
        out_kl[i : i + 1, :] = divergence[:, i * span : (i + 1) * span]


def on_device(sizes, hidden, policy_head, reference_head, targets, loss_mask):
    vocab, section = sizes
    A, B = split_axis(vocab)
    X, C = split_axis(section)
    piece, width = hidden.shape[1], hidden.shape[2]
    tokens = targets.size
    gathers = (X - 1) + (B - 1) + 2 * (X - 1) * (B - 1)
    anywhere = pl.BlockSpec(memory_space=pl.ANY)
    vmem = pl.BlockSpec(memory_space=pltpu.VMEM)
    heads = policy_head.size + reference_head.size
    moments = pl.pallas_call(
        functools.partial(kernel, sizes),
        out_shape=jax.ShapeDtypeStruct((8, tokens), jnp.float32),
        in_specs=[anywhere, anywhere, anywhere, vmem],
        out_specs=vmem,
        scratch_shapes=[
            pltpu.VMEM((A, piece, width), hidden.dtype),
            pltpu.VMEM((B * X * C, A * piece, width), hidden.dtype),
            pltpu.VMEM(policy_head.shape, policy_head.dtype),
            pltpu.VMEM(reference_head.shape, reference_head.dtype),
            pltpu.VMEM((policy_head.shape[0], tokens), jnp.float32),
            pltpu.VMEM((reference_head.shape[0], tokens), jnp.float32),
            pltpu.VMEM((B * X * C, 16, tokens), jnp.float32),
            pltpu.VMEM((A, 16, tokens), jnp.float32),
            pltpu.SemaphoreType.DMA((3,)),
            pltpu.SemaphoreType.DMA((1,)),
            pltpu.SemaphoreType.DMA((PARTS,)),
            pltpu.SemaphoreType.DMA((1,)),
            pltpu.SemaphoreType.DMA((PARTS,)),
            pltpu.SemaphoreType.DMA((PARTS * gathers,)),
            pltpu.SemaphoreType.DMA((2,)),
            pltpu.SemaphoreType.DMA((2,)),
        ],
        compiler_params=pltpu.CompilerParams(
            collective_id=0, has_side_effects=True, vmem_limit_bytes=60 * 1024 * 1024
        ),
        cost_estimate=pl.CostEstimate(
            flops=2 * tokens * heads, bytes_accessed=2 * heads, transcendentals=3 * tokens * policy_head.shape[0]
        ),
    )(hidden, policy_head, reference_head, targets)
    return pl.pallas_call(
        functools.partial(finish, A, B),
        out_shape=(
            jax.ShapeDtypeStruct(targets.shape, jnp.float32),
            jax.ShapeDtypeStruct(targets.shape, jnp.float32),
            jax.ShapeDtypeStruct((3,), jnp.float32),
        ),
        in_specs=[vmem, vmem],
        out_specs=(vmem, vmem, pl.BlockSpec(memory_space=pltpu.SMEM)),
    )(moments, loss_mask)


def solution(mesh):
    placed = (
        P("section", "vocab", None),
        P(("vocab", "section"), None),
        P(("vocab", "section"), None),
        P(),
        P(),
    )
    sizes = (mesh.shape["vocab"], mesh.shape["section"])
    return jax.shard_map(
        functools.partial(on_device, sizes),
        mesh=mesh, in_specs=placed, out_specs=(P(), P(), P()), check_vma=False,
    )
```

```python
import functools
import itertools

import jax
import jax.numpy as jnp
from jax import lax
from jax.experimental import pallas as pl
from jax.experimental.pallas import tpu as pltpu
from jax.sharding import PartitionSpec as P

MESH = pl.DeviceIdType.MESH


def split_axis(size):
    return (size // 2, 2) if size % 2 == 0 else (size, 1)


def power_of_two(size):
    return size & (size - 1) == 0


def flip(index, step, size):
    result = index
    bit = 1
    while bit < size:
        if step & bit:
            result = result + bit - 2 * bit * ((index // bit) % 2)
        bit *= 2
    return result


def target_of(index, step, size):
    if step == 0:
        return index
    return flip(index, step, size) if power_of_two(size) else (index + step) % size


def source_of(index, step, size):
    if step == 0:
        return index
    return flip(index, step, size) if power_of_two(size) else (index + size - step) % size


def merge(parts):
    top = functools.reduce(jnp.maximum, [part[8:16] for part in parts])
    total = sum(jnp.exp(part[8:16] - top) * part[0:8] for part in parts)
    return total, top


def to_groups(values, A, B, piece):
    return jnp.concatenate(
        [
            values[m : m + 1, (i * B + j) * piece : (i * B + j + 1) * piece]
            for m in range(values.shape[0]) for j in range(B) for i in range(A)
        ],
        axis=1,
    )


def from_groups(values, micro, A, B, piece):
    starts = [((m * B + j) * A + i) * piece for m in range(micro) for i in range(A) for j in range(B)]
    return jnp.concatenate([values[:, at : at + piece] for at in starts], axis=1)


PARTS = 4
STEPS = 1


def kernel(
    sizes, hid, hp, hr, tgt, out,
    strip, rows, wp, wr, plog_acc, rlog_acc, plane, line,
    local_sem, strip_sent, strip_sem, rows_sent, core_sem, recv_sem, stat_sent, stat_sem,
):
    vocab, section = sizes
    A, B = split_axis(vocab)
    X, C = split_axis(section)
    v, s = lax.axis_index("vocab"), lax.axis_index("section")
    a, b = v // B, v % B
    x, c = s // C, s % C
    dims = (A, B, X, C)
    here = (a, b, x, c)
    piece, width = hid.shape[1], hid.shape[2]
    groups, high = rows.shape[0], rows.shape[1]
    tokens = groups * high
    count = wp.shape[0]
    share_width = width // PARTS
    step_width = share_width // STEPS
    bundle = 128 // high if tokens % 128 == 0 and 128 % high == 0 else groups
    tile = bundle * high

    def device(at):
        return (at[0] * B + at[1], at[2] * C + at[3])

    def group(at):
        return (at[2] * C + at[3]) * B + at[1]

    def to(step):
        return tuple(target_of(i, d, n) for i, d, n in zip(here, step, dims))

    def back(step):
        return tuple(source_of(i, d, n) for i, d, n in zip(here, step, dims))

    line_steps = [(d, 0, 0, 0) for d in range(1, A)]
    plane_steps = [(0,) + e for e in itertools.product(range(B), range(X), range(C)) if any(e)]
    barrier = pltpu.get_barrier_semaphore()
    for step in line_steps + plane_steps:
        pl.semaphore_signal(barrier, inc=1, device_id=device(to(step)), device_id_type=MESH)

    own = pltpu.make_async_copy(hid.at[0], strip.at[a], local_sem.at[0])
    own.start()
    load_p = pltpu.make_async_copy(hp, wp, local_sem.at[1])
    load_p.start()
    load_r = pltpu.make_async_copy(hr, wr, local_sem.at[2])
    load_r.start()
    wanted = to_groups(tgt[...], A, B, piece)
    own.wait()
    pl.semaphore_wait(barrier, len(line_steps) + len(plane_steps))

    keys = {}

    def view(at, h, half):
        lo, size = h * share_width, share_width
        if half is not None:
            size = share_width // 2
            lo = lo + half * size
        return rows.at[group(at), :, pl.ds(lo, size)]

    def describe(key, step, at, h, half):
        part = view(at, h, half)
        if key[0] == "core":
            arrived = core_sem.at[h]
        else:
            arrived = recv_sem.at[keys.setdefault((h,) + key, len(keys))]
        return pltpu.make_async_remote_copy(
            src_ref=part, dst_ref=part, send_sem=rows_sent.at[0], recv_sem=arrived,
            device_id=device(to(step)), device_id_type=MESH,
        )

    def copy(key, step, at, h, half=None):
        describe(key, step, at, h, half).start()

    def arrive(key, step, at, h, half=None):
        describe(key, step, at, h, half).wait_recv()

    def to_cores(step, h):
        for dc in range(1, C):
            copy(("core", step, dc), (0, 0, 0, dc), back(step), h)

    def send_strip(h):
        part = strip.at[a, :, pl.ds(h * share_width, share_width)]
        for step in line_steps:
            pltpu.make_async_remote_copy(
                src_ref=part, dst_ref=part, send_sem=strip_sent.at[0], recv_sem=strip_sem.at[h],
                device_id=device(to(step)), device_id_type=MESH,
            ).start()

    def fan(h):
        columns = pl.ds(h * share_width, share_width)
        if A > 1:
            part = strip.at[pl.ds(0, A - 1), :, columns]
            pltpu.make_async_copy(part, part, strip_sem.at[h]).wait()
        rows[group(here), :, columns] = jnp.concatenate(
            [strip[i, :, columns] for i in range(A)], axis=0
        )
        for dx in range(1, X):
            copy(("x", dx), (0, 0, dx, 0), here, h)
        for db in range(1, B):
            copy(("b", db), (0, db, 0, 0), here, h)
        to_cores((0, 0, 0, 0), h)

    def cross(h):
        for dx in range(1, X):
            at = back((0, 0, dx, 0))
            arrive(("x", dx), (0, 0, dx, 0), at, h)
            for db in range(1, B):
                copy(("xb", dx, db), (0, db, 0, 0), at, h, 0)
        for db in range(1, B):
            at = back((0, db, 0, 0))
            arrive(("b", db), (0, db, 0, 0), at, h)
            for dx in range(1, X):
                copy(("bx", dx, db), (0, 0, dx, 0), at, h, 1)
        for dx in range(1, X):
            to_cores((0, 0, dx, 0), h)
        for db in range(1, B):
            to_cores((0, db, 0, 0), h)

    def corner(h):
        for dx in range(1, X):
            for db in range(1, B):
                at = back((0, db, dx, 0))
                arrive(("xb", dx, db), (0, db, 0, 0), at, h, 0)
                arrive(("bx", dx, db), (0, 0, dx, 0), at, h, 1)
                to_cores((0, db, dx, 0), h)

    def from_cores(h):
        if C > 1:
            part = rows.at[pl.ds(0, groups // C * (C - 1)), :, pl.ds(0, share_width)]
            pltpu.make_async_copy(part, part, core_sem.at[h]).wait()

    dims_nt = (((1,), (1,)), ((), ()))

    def multiply(k):
        columns = pl.ds(k * step_width, step_width)

        def tile_of(n):
            mine = rows[pl.ds(n * bundle, bundle), :, columns].reshape(tile, step_width)
            place = pl.ds(n * tile if isinstance(n, int) else pl.multiple_of(n * tile, tile), tile)
            for head, total in ((wp, plog_acc), (wr, rlog_acc)):
                logits = lax.dot_general(
                    head[:, columns], mine, dims_nt, preferred_element_type=jnp.float32
                )
                if k == 0:
                    total[:, place] = logits
                else:
                    total[:, place] += logits

        if tokens == tile:
            tile_of(0)
        else:
            pl.loop(0, tokens // tile)(tile_of)

    for h in range(PARTS):
        send_strip(h)
    for u in range(PARTS + 1):
        if u < PARTS:
            fan(u)
        if 1 <= u:
            cross(u - 1)
        if 2 <= u:
            corner(u - 2)
    load_p.wait()
    load_r.wait()
    early = (PARTS - 1) * STEPS
    for k in range(PARTS * STEPS):
        if k == (early + 1) // 2:
            corner(PARTS - 1)
        if k % STEPS == 0:
            from_cores(k // STEPS)
        multiply(k)

    offset = (v * section + s) * count
    moments = []
    for n in range(tokens // tile):
        place = slice(n * tile, (n + 1) * tile)
        plog, rlog = plog_acc[:, place], rlog_acc[:, place]
        top = jnp.max(plog, axis=0, keepdims=True)
        shift = plog - top
        weight = jnp.exp(shift)
        total = jnp.sum(weight, axis=0, keepdims=True)
        first = jnp.sum(weight * plog, axis=0, keepdims=True)
        across = jnp.sum(weight * (plog - rlog), axis=0, keepdims=True)
        ids = offset + lax.broadcasted_iota(jnp.int32, plog.shape, 0)
        chosen = jnp.sum(jnp.where(ids == wanted[:, place], plog, 0.0), axis=0, keepdims=True)
        rtop = jnp.max(rlog, axis=0, keepdims=True)
        rtotal = jnp.sum(jnp.exp(rlog - rtop), axis=0, keepdims=True)
        none = jnp.zeros_like(top)
        moments.append(
            jnp.concatenate(
                [total, first, across, rtotal, chosen, none, none, none]
                + [top, top, top, rtop, none, none, none, none],
                axis=0,
            )
        )
    index = b * (X * C) + x * C + c
    plane[index] = jnp.concatenate(moments, axis=1) if len(moments) > 1 else moments[0]

    def exchange(i, steps, buffer, position):
        part = buffer.at[position]
        for step in steps:
            pltpu.make_async_remote_copy(
                src_ref=part, dst_ref=part, send_sem=stat_sent.at[i], recv_sem=stat_sem.at[i],
                device_id=device(to(step)), device_id_type=MESH,
            ).start()

    def exchanged(i, steps, buffer, sem):
        if steps:
            part = buffer.at[pl.ds(0, len(steps))]
            pltpu.make_async_copy(part, part, sem.at[i]).wait()

    exchange(0, plane_steps, plane, index)
    if A > 1:
        sent = strip.at[pl.ds(0, A - 1)]
        pltpu.make_async_copy(sent, sent, strip_sent.at[0]).wait()
    if groups > 1:
        sent = rows.at[pl.ds(0, groups - 1)]
        pltpu.make_async_copy(sent, sent, rows_sent.at[0]).wait()
    exchanged(0, plane_steps, plane, stat_sem)
    line[a] = jnp.concatenate(merge([plane[i] for i in range(B * X * C)]), axis=0)
    exchange(1, line_steps, line, a)
    exchanged(0, plane_steps, plane, stat_sent)
    exchanged(1, line_steps, line, stat_sem)
    total, top = merge([line[i] for i in range(A)])
    out[...] = jnp.concatenate([total[0:5], top[0:1], top[3:4], total[7:8]], axis=0)
    exchanged(1, line_steps, line, stat_sent)


def finish(A, B, stats, msk, out_lp, out_kl, out_tot):
    micro, span = msk.shape
    ordered = from_groups(stats[...], micro, A, B, span // (A * B))
    total, first, across, rtotal, chosen, top, rtop = [ordered[i : i + 1, :] for i in range(7)]
    lse = top + jnp.log(total)
    logprob = chosen - lse
    entropy = lse - first / total
    divergence = across / total - lse + (rtop + jnp.log(rtotal))
    mask = jnp.concatenate([msk[i : i + 1, :] for i in range(micro)], axis=1).astype(jnp.float32)
    scale = 1.0 / (micro * span)
    out_tot[0] = jnp.sum(mask * logprob) * scale
    out_tot[1] = jnp.sum(mask * entropy) * scale
    out_tot[2] = jnp.sum(mask * divergence) * scale
    for i in range(micro):
        out_lp[i : i + 1, :] = logprob[:, i * span : (i + 1) * span]
        out_kl[i : i + 1, :] = divergence[:, i * span : (i + 1) * span]


def on_device(sizes, hidden, policy_head, reference_head, targets, loss_mask):
    vocab, section = sizes
    A, B = split_axis(vocab)
    X, C = split_axis(section)
    piece, width = hidden.shape[1], hidden.shape[2]
    tokens = targets.size
    gathers = (X - 1) + (B - 1) + 2 * (X - 1) * (B - 1)
    anywhere = pl.BlockSpec(memory_space=pl.ANY)
    vmem = pl.BlockSpec(memory_space=pltpu.VMEM)
    heads = policy_head.size + reference_head.size
    moments = pl.pallas_call(
        functools.partial(kernel, sizes),
        out_shape=jax.ShapeDtypeStruct((8, tokens), jnp.float32),
        in_specs=[anywhere, anywhere, anywhere, vmem],
        out_specs=vmem,
        scratch_shapes=[
            pltpu.VMEM((A, piece, width), hidden.dtype),
            pltpu.VMEM((B * X * C, A * piece, width), hidden.dtype),
            pltpu.VMEM(policy_head.shape, policy_head.dtype),
            pltpu.VMEM(reference_head.shape, reference_head.dtype),
            pltpu.VMEM((policy_head.shape[0], tokens), jnp.float32),
            pltpu.VMEM((reference_head.shape[0], tokens), jnp.float32),
            pltpu.VMEM((B * X * C, 16, tokens), jnp.float32),
            pltpu.VMEM((A, 16, tokens), jnp.float32),
            pltpu.SemaphoreType.DMA((3,)),
            pltpu.SemaphoreType.DMA((1,)),
            pltpu.SemaphoreType.DMA((PARTS,)),
            pltpu.SemaphoreType.DMA((1,)),
            pltpu.SemaphoreType.DMA((PARTS,)),
            pltpu.SemaphoreType.DMA((PARTS * gathers,)),
            pltpu.SemaphoreType.DMA((2,)),
            pltpu.SemaphoreType.DMA((2,)),
        ],
        compiler_params=pltpu.CompilerParams(
            collective_id=0, has_side_effects=True, vmem_limit_bytes=60 * 1024 * 1024
        ),
        cost_estimate=pl.CostEstimate(
            flops=2 * tokens * heads, bytes_accessed=2 * heads, transcendentals=3 * tokens * policy_head.shape[0]
        ),
    )(hidden, policy_head, reference_head, targets)
    return pl.pallas_call(
        functools.partial(finish, A, B),
        out_shape=(
            jax.ShapeDtypeStruct(targets.shape, jnp.float32),
            jax.ShapeDtypeStruct(targets.shape, jnp.float32),
            jax.ShapeDtypeStruct((3,), jnp.float32),
        ),
        in_specs=[vmem, vmem],
        out_specs=(vmem, vmem, pl.BlockSpec(memory_space=pltpu.SMEM)),
    )(moments, loss_mask)


def solution(mesh):
    placed = (
        P("section", "vocab", None),
        P(("vocab", "section"), None),
        P(("vocab", "section"), None),
        P(),
        P(),
    )
    sizes = (mesh.shape["vocab"], mesh.shape["section"])
    return jax.shard_map(
        functools.partial(on_device, sizes),
        mesh=mesh, in_specs=placed, out_specs=(P(), P(), P()), check_vma=False,
    )
```

```python
import functools
import itertools

import jax
import jax.numpy as jnp
from jax import lax
from jax.experimental import pallas as pl
from jax.experimental.pallas import tpu as pltpu
from jax.sharding import PartitionSpec as P

MESH = pl.DeviceIdType.MESH


def split_axis(size):
    return (size // 2, 2) if size % 2 == 0 else (size, 1)


def power_of_two(size):
    return size & (size - 1) == 0


def flip(index, step, size):
    result = index
    bit = 1
    while bit < size:
        if step & bit:
            result = result + bit - 2 * bit * ((index // bit) % 2)
        bit *= 2
    return result


def target_of(index, step, size):
    if step == 0:
        return index
    return flip(index, step, size) if power_of_two(size) else (index + step) % size


def source_of(index, step, size):
    if step == 0:
        return index
    return flip(index, step, size) if power_of_two(size) else (index + size - step) % size


def merge(buffer):
    parts = range(buffer.shape[0])
    top = functools.reduce(jnp.maximum, [buffer[i, 5:6, :] for i in parts])
    rtop = functools.reduce(jnp.maximum, [buffer[i, 6:7, :] for i in parts])
    row = lax.broadcasted_iota(jnp.int32, buffer.shape[1:], 0)
    total = jnp.zeros(buffer.shape[1:], buffer.dtype)
    for i in parts:
        shift = jnp.where(row == 3, buffer[i, 6:7, :] - rtop, 0.0)
        shift = jnp.where(row < 3, buffer[i, 5:6, :] - top, shift)
        total = total + jnp.exp(shift) * buffer[i]
    return jnp.where(row == 5, top, jnp.where(row == 6, rtop, total))


def to_groups(values, A, B, piece):
    return jnp.concatenate(
        [
            values[m : m + 1, (i * B + j) * piece : (i * B + j + 1) * piece]
            for m in range(values.shape[0]) for j in range(B) for i in range(A)
        ],
        axis=1,
    )


def from_groups(values, micro, A, B, piece):
    starts = [((m * B + j) * A + i) * piece for m in range(micro) for i in range(A) for j in range(B)]
    return jnp.concatenate([values[:, at : at + piece] for at in starts], axis=1)


PARTS = 2
STEPS = 2


def kernel(
    sizes, hid, hp, hr, tgt, out,
    strip, rows, wp, wr, plog_acc, rlog_acc, plane, line,
    local_sem, strip_sent, strip_sem, rows_sent, core_sem, recv_sem, stat_sent, stat_sem,
):
    vocab, section = sizes
    A, B = split_axis(vocab)
    X, C = split_axis(section)
    v, s = lax.axis_index("vocab"), lax.axis_index("section")
    a, b = v // B, v % B
    x, c = s // C, s % C
    dims = (A, B, X, C)
    here = (a, b, x, c)
    piece, width = hid.shape[1], hid.shape[2]
    groups, high = rows.shape[0], rows.shape[1]
    tokens = groups * high
    count = wp.shape[0]
    share_width = width // PARTS
    step_width = share_width // STEPS
    bundle = 128 // high if tokens % 128 == 0 and 128 % high == 0 else groups
    tile = bundle * high

    def device(at):
        return (at[0] * B + at[1], at[2] * C + at[3])

    def group(at):
        return (at[2] * C + at[3]) * B + at[1]

    def to(step):
        return tuple(target_of(i, d, n) for i, d, n in zip(here, step, dims))

    def back(step):
        return tuple(source_of(i, d, n) for i, d, n in zip(here, step, dims))

    own = pltpu.make_async_copy(hid.at[0], strip.at[a], local_sem.at[0])
    own.start()
    line_steps = [(d, 0, 0, 0) for d in range(1, A)]
    plane_steps = [(0,) + e for e in itertools.product(range(B), range(X), range(C)) if any(e)]
    barrier = pltpu.get_barrier_semaphore()
    for step in line_steps + plane_steps:
        pl.semaphore_signal(barrier, inc=1, device_id=device(to(step)), device_id_type=MESH)

    load_p = pltpu.make_async_copy(hp, wp, local_sem.at[1])
    load_p.start()
    load_r = pltpu.make_async_copy(hr, wr, local_sem.at[2])
    load_r.start()
    pl.semaphore_wait(barrier, len(line_steps) + len(plane_steps))

    keys = {}

    def view(at, h, half):
        lo, size = h * share_width, share_width
        if half is not None:
            size = share_width // 2
            lo = lo + half * size
        return rows.at[group(at), :, pl.ds(lo, size)]

    def describe(key, step, at, h, half):
        part = view(at, h, half)
        if key[0] == "core":
            arrived = core_sem.at[h]
        else:
            arrived = recv_sem.at[keys.setdefault((h,) + key, len(keys))]
        return pltpu.make_async_remote_copy(
            src_ref=part, dst_ref=part, send_sem=rows_sent.at[0], recv_sem=arrived,
            device_id=device(to(step)), device_id_type=MESH,
        )

    def copy(key, step, at, h, half=None):
        describe(key, step, at, h, half).start()

    def arrive(key, step, at, h, half=None):
        describe(key, step, at, h, half).wait_recv()

    def to_cores(step, h):
        for dc in range(1, C):
            copy(("core", step, dc), (0, 0, 0, dc), back(step), h)

    def send_strip(h):
        columns = pl.ds(h * share_width, share_width)
        for step in line_steps:
            pltpu.make_async_remote_copy(
                src_ref=hid.at[0, :, columns], dst_ref=strip.at[a, :, columns], send_sem=strip_sent.at[0], recv_sem=strip_sem.at[h],
                device_id=device(to(step)), device_id_type=MESH,
            ).start()

    def fan(h):
        columns = pl.ds(h * share_width, share_width)
        if A > 1:
            part = strip.at[pl.ds(0, A - 1), :, columns]
            pltpu.make_async_copy(part, part, strip_sem.at[h]).wait()
        rows[group(here), :, columns] = jnp.concatenate(
            [strip[i, :, columns] for i in range(A)], axis=0
        )
        for dx in range(1, X):
            copy(("x", dx), (0, 0, dx, 0), here, h)
        for db in range(1, B):
            copy(("b", db), (0, db, 0, 0), here, h)
        to_cores((0, 0, 0, 0), h)

    def cross(h):
        for dx in range(1, X):
            at = back((0, 0, dx, 0))
            arrive(("x", dx), (0, 0, dx, 0), at, h)
            for db in range(1, B):
                copy(("xb", dx, db), (0, db, 0, 0), at, h, 0)
        for db in range(1, B):
            at = back((0, db, 0, 0))
            arrive(("b", db), (0, db, 0, 0), at, h)
            for dx in range(1, X):
                copy(("bx", dx, db), (0, 0, dx, 0), at, h, 1)
        for dx in range(1, X):
            to_cores((0, 0, dx, 0), h)
        for db in range(1, B):
            to_cores((0, db, 0, 0), h)

    def corner(h):
        for dx in range(1, X):
            for db in range(1, B):
                at = back((0, db, dx, 0))
                arrive(("xb", dx, db), (0, db, 0, 0), at, h, 0)
                arrive(("bx", dx, db), (0, 0, dx, 0), at, h, 1)
                to_cores((0, db, dx, 0), h)

    def from_cores(h):
        if C > 1:
            part = rows.at[pl.ds(0, groups // C * (C - 1)), :, pl.ds(0, share_width)]
            pltpu.make_async_copy(part, part, core_sem.at[h]).wait()

    dims_nt = (((1,), (1,)), ((), ()))

    def multiply(k):
        columns = pl.ds(k * step_width, step_width)

        def tile_of(n):
            mine = rows[pl.ds(n * bundle, bundle), :, columns].reshape(tile, step_width)
            place = pl.ds(n * tile if isinstance(n, int) else pl.multiple_of(n * tile, tile), tile)
            for head, total in ((wp, plog_acc), (wr, rlog_acc)):
                logits = lax.dot_general(
                    head[:, columns], mine, dims_nt, preferred_element_type=jnp.float32
                )
                if k == 0:
                    total[:, place] = logits
                else:
                    total[:, place] += logits

        if tokens == tile:
            tile_of(0)
        else:
            pl.loop(0, tokens // tile)(tile_of)

    for h in range(PARTS):
        send_strip(h)
    wanted = to_groups(tgt[...], A, B, piece)
    own.wait()
    for u in range(PARTS + 1):
        if u < PARTS:
            fan(u)
        if 1 <= u:
            cross(u - 1)
        if 2 <= u:
            corner(u - 2)
    load_p.wait()
    load_r.wait()
    early = (PARTS - 1) * STEPS
    for k in range(PARTS * STEPS):
        if k == (early + 1) // 2:
            corner(PARTS - 1)
        if k % STEPS == 0:
            from_cores(k // STEPS)
        multiply(k)

    offset = (v * section + s) * count
    moments = []
    for n in range(tokens // tile):
        place = slice(n * tile, (n + 1) * tile)
        plog, rlog = plog_acc[:, place], rlog_acc[:, place]
        top = jnp.max(plog, axis=0, keepdims=True)
        shift = plog - top
        weight = jnp.exp(shift)
        total = jnp.sum(weight, axis=0, keepdims=True)
        first = jnp.sum(weight * plog, axis=0, keepdims=True)
        across = jnp.sum(weight * (plog - rlog), axis=0, keepdims=True)
        ids = offset + lax.broadcasted_iota(jnp.int32, plog.shape, 0)
        chosen = jnp.sum(jnp.where(ids == wanted[:, place], plog, 0.0), axis=0, keepdims=True)
        rtop = jnp.max(rlog, axis=0, keepdims=True)
        rtotal = jnp.sum(jnp.exp(rlog - rtop), axis=0, keepdims=True)
        none = jnp.zeros_like(top)
        moments.append(
            jnp.concatenate(
                [total, first, across, rtotal, chosen, top, rtop, none], axis=0
            )
        )
    index = b * (X * C) + x * C + c
    plane[index] = jnp.concatenate(moments, axis=1) if len(moments) > 1 else moments[0]

    def exchange(i, steps, buffer, position):
        part = buffer.at[position]
        for step in steps:
            pltpu.make_async_remote_copy(
                src_ref=part, dst_ref=part, send_sem=stat_sent.at[i], recv_sem=stat_sem.at[i],
                device_id=device(to(step)), device_id_type=MESH,
            ).start()

    def exchanged(i, steps, buffer, sem):
        if steps:
            part = buffer.at[pl.ds(0, len(steps))]
            pltpu.make_async_copy(part, part, sem.at[i]).wait()

    exchange(0, plane_steps, plane, index)
    if A > 1:
        sent = strip.at[pl.ds(0, A - 1)]
        pltpu.make_async_copy(sent, sent, strip_sent.at[0]).wait()
    if groups > 1:
        sent = rows.at[pl.ds(0, groups - 1)]
        pltpu.make_async_copy(sent, sent, rows_sent.at[0]).wait()
    exchanged(0, plane_steps, plane, stat_sem)
    line[a] = merge(plane)
    exchange(1, line_steps, line, a)
    exchanged(0, plane_steps, plane, stat_sent)
    exchanged(1, line_steps, line, stat_sem)
    out[...] = merge(line)
    exchanged(1, line_steps, line, stat_sent)


def finish(A, B, stats, msk, out_lp, out_kl, out_tot):
    micro, span = msk.shape
    ordered = from_groups(stats[...], micro, A, B, span // (A * B))
    total, first, across, rtotal, chosen, top, rtop = [ordered[i : i + 1, :] for i in range(7)]
    lse = top + jnp.log(total)
    logprob = chosen - lse
    entropy = lse - first / total
    divergence = across / total - lse + (rtop + jnp.log(rtotal))
    mask = jnp.concatenate([msk[i : i + 1, :] for i in range(micro)], axis=1).astype(jnp.float32)
    scale = 1.0 / (micro * span)
    out_tot[0] = jnp.sum(mask * logprob) * scale
    out_tot[1] = jnp.sum(mask * entropy) * scale
    out_tot[2] = jnp.sum(mask * divergence) * scale
    for i in range(micro):
        out_lp[i : i + 1, :] = logprob[:, i * span : (i + 1) * span]
        out_kl[i : i + 1, :] = divergence[:, i * span : (i + 1) * span]


def on_device(sizes, hidden, policy_head, reference_head, targets, loss_mask):
    vocab, section = sizes
    A, B = split_axis(vocab)
    X, C = split_axis(section)
    piece, width = hidden.shape[1], hidden.shape[2]
    tokens = targets.size
    gathers = (X - 1) + (B - 1) + 2 * (X - 1) * (B - 1)
    anywhere = pl.BlockSpec(memory_space=pl.ANY)
    vmem = pl.BlockSpec(memory_space=pltpu.VMEM)
    heads = policy_head.size + reference_head.size
    moments = pl.pallas_call(
        functools.partial(kernel, sizes),
        out_shape=jax.ShapeDtypeStruct((8, tokens), jnp.float32),
        in_specs=[anywhere, anywhere, anywhere, vmem],
        out_specs=vmem,
        scratch_shapes=[
            pltpu.VMEM((A, piece, width), hidden.dtype),
            pltpu.VMEM((B * X * C, A * piece, width), hidden.dtype),
            pltpu.VMEM(policy_head.shape, policy_head.dtype),
            pltpu.VMEM(reference_head.shape, reference_head.dtype),
            pltpu.VMEM((policy_head.shape[0], tokens), jnp.float32),
            pltpu.VMEM((reference_head.shape[0], tokens), jnp.float32),
            pltpu.VMEM((B * X * C, 8, tokens), jnp.float32),
            pltpu.VMEM((A, 8, tokens), jnp.float32),
            pltpu.SemaphoreType.DMA((3,)),
            pltpu.SemaphoreType.DMA((1,)),
            pltpu.SemaphoreType.DMA((PARTS,)),
            pltpu.SemaphoreType.DMA((1,)),
            pltpu.SemaphoreType.DMA((PARTS,)),
            pltpu.SemaphoreType.DMA((PARTS * gathers,)),
            pltpu.SemaphoreType.DMA((2,)),
            pltpu.SemaphoreType.DMA((2,)),
        ],
        compiler_params=pltpu.CompilerParams(
            collective_id=0, has_side_effects=True, vmem_limit_bytes=60 * 1024 * 1024
        ),
        cost_estimate=pl.CostEstimate(
            flops=2 * tokens * heads, bytes_accessed=2 * heads, transcendentals=3 * tokens * policy_head.shape[0]
        ),
    )(hidden, policy_head, reference_head, targets)
    return pl.pallas_call(
        functools.partial(finish, A, B),
        out_shape=(
            jax.ShapeDtypeStruct(targets.shape, jnp.float32),
            jax.ShapeDtypeStruct(targets.shape, jnp.float32),
            jax.ShapeDtypeStruct((3,), jnp.float32),
        ),
        in_specs=[vmem, vmem],
        out_specs=(vmem, vmem, pl.BlockSpec(memory_space=pltpu.SMEM)),
    )(moments, loss_mask)


def solution(mesh):
    placed = (
        P("section", "vocab", None),
        P(("vocab", "section"), None),
        P(("vocab", "section"), None),
        P(),
        P(),
    )
    sizes = (mesh.shape["vocab"], mesh.shape["section"])
    return jax.shard_map(
        functools.partial(on_device, sizes),
        mesh=mesh, in_specs=placed, out_specs=(P(), P(), P()), check_vma=False,
    )
```

```python
import functools
import itertools

import jax
import jax.numpy as jnp
from jax import lax
from jax.experimental import pallas as pl
from jax.experimental.pallas import tpu as pltpu
from jax.sharding import PartitionSpec as P

MESH = pl.DeviceIdType.MESH


def split_axis(size):
    return (size // 2, 2) if size % 2 == 0 else (size, 1)


def power_of_two(size):
    return size & (size - 1) == 0


def flip(index, step, size):
    result = index
    bit = 1
    while bit < size:
        if step & bit:
            result = result + bit - 2 * bit * lax.rem(lax.div(index, bit), 2)
        bit *= 2
    return result


def target_of(index, step, size):
    if step == 0:
        return index
    return flip(index, step, size) if power_of_two(size) else lax.rem(index + step, size)


def source_of(index, step, size):
    if step == 0:
        return index
    return flip(index, step, size) if power_of_two(size) else lax.rem(index + size - step, size)


def merge(buffer):
    parts = range(buffer.shape[0])
    top = functools.reduce(jnp.maximum, [buffer[i, 5:6, :] for i in parts])
    rtop = functools.reduce(jnp.maximum, [buffer[i, 6:7, :] for i in parts])
    row = lax.broadcasted_iota(jnp.int32, buffer.shape[1:], 0)
    total = jnp.zeros(buffer.shape[1:], buffer.dtype)
    for i in parts:
        shift = jnp.where(row == 3, buffer[i, 6:7, :] - rtop, 0.0)
        shift = jnp.where(row < 3, buffer[i, 5:6, :] - top, shift)
        total = total + jnp.exp(shift) * buffer[i]
    return jnp.where(row == 5, top, jnp.where(row == 6, rtop, total))


def to_groups(values, A, B, piece):
    return jnp.concatenate(
        [
            values[m : m + 1, (i * B + j) * piece : (i * B + j + 1) * piece]
            for m in range(values.shape[0]) for j in range(B) for i in range(A)
        ],
        axis=1,
    )


def from_groups(values, micro, A, B, piece):
    starts = [((m * B + j) * A + i) * piece for m in range(micro) for i in range(A) for j in range(B)]
    return jnp.concatenate([values[:, at : at + piece] for at in starts], axis=1)


PARTS = 4
STEPS = 1


def kernel(
    sizes, hid, hp, hr, tgt, out,
    strip, rows, wp, wr, plog_acc, rlog_acc, plane, line,
    local_sem, strip_sent, strip_sem, rows_sent, core_sem, recv_sem, stat_sent, stat_sem,
):
    vocab, section = sizes
    A, B = split_axis(vocab)
    X, C = split_axis(section)
    v, s = lax.axis_index("vocab"), lax.axis_index("section")
    a, b = lax.div(v, B), lax.rem(v, B)
    x, c = lax.div(s, C), lax.rem(s, C)
    dims = (A, B, X, C)
    here = (a, b, x, c)
    piece, width = hid.shape[1], hid.shape[2]
    groups, high = rows.shape[0], rows.shape[1]
    tokens = groups * high
    count = wp.shape[0]
    share_width = width // PARTS
    step_width = share_width // STEPS
    bundle = 128 // high if tokens % 128 == 0 and 128 % high == 0 else groups
    tile = bundle * high

    def device(at):
        return (at[0] * B + at[1], at[2] * C + at[3])

    def group(at):
        return (at[2] * C + at[3]) * B + at[1]

    outward = [[target_of(i, d, n) for d in range(n)] for i, n in zip(here, dims)]
    inward = [[source_of(i, d, n) for d in range(n)] for i, n in zip(here, dims)]

    def to(step):
        return tuple(known[d] for known, d in zip(outward, step))

    def back(step):
        return tuple(known[d] for known, d in zip(inward, step))

    own = pltpu.make_async_copy(hid.at[0], strip.at[a], local_sem.at[0])
    own.start()
    line_steps = [(d, 0, 0, 0) for d in range(1, A)]
    plane_steps = [(0,) + e for e in itertools.product(range(B), range(X), range(C)) if any(e)]
    barrier = pltpu.get_barrier_semaphore()
    for step in line_steps + plane_steps:
        pl.semaphore_signal(barrier, inc=1, device_id=device(to(step)), device_id_type=MESH)

    load_p = pltpu.make_async_copy(hp, wp, local_sem.at[1])
    load_p.start()
    load_r = pltpu.make_async_copy(hr, wr, local_sem.at[2])
    load_r.start()
    pl.semaphore_wait(barrier, len(line_steps) + len(plane_steps))

    keys = {}

    def view(at, h, half):
        lo, size = h * share_width, share_width
        if half is not None:
            size = share_width // 2
            lo = lo + half * size
        return rows.at[group(at), :, pl.ds(lo, size)]

    def describe(key, step, at, h, half):
        part = view(at, h, half)
        arrived = recv_sem.at[keys.setdefault((h,) + key, len(keys))]
        return pltpu.make_async_remote_copy(
            src_ref=part, dst_ref=part, send_sem=rows_sent.at[0], recv_sem=arrived,
            device_id=device(to(step)), device_id_type=MESH,
        )

    def copy(key, step, at, h, half=None):
        describe(key, step, at, h, half).start()

    def arrive(key, step, at, h, half=None):
        describe(key, step, at, h, half).wait_recv()

    def to_cores(dx, h):
        first = (back((0, 0, dx, 0))[2] * C + c) * B
        part = rows.at[pl.ds(first, B), :, pl.ds(h * share_width, share_width)]
        for dc in range(1, C):
            pltpu.make_async_remote_copy(
                src_ref=part, dst_ref=part, send_sem=rows_sent.at[0], recv_sem=core_sem.at[h],
                device_id=device(to((0, 0, 0, dc))), device_id_type=MESH,
            ).start()

    def send_strip(h):
        columns = pl.ds(h * share_width, share_width)
        for step in line_steps:
            pltpu.make_async_remote_copy(
                src_ref=hid.at[0, :, columns], dst_ref=strip.at[a, :, columns], send_sem=strip_sent.at[0], recv_sem=strip_sem.at[h],
                device_id=device(to(step)), device_id_type=MESH,
            ).start()

    def fan(h):
        columns = pl.ds(h * share_width, share_width)
        if A > 1:
            part = strip.at[pl.ds(0, A - 1), :, columns]
            pltpu.make_async_copy(part, part, strip_sem.at[h]).wait()
        rows[group(here), :, columns] = jnp.concatenate(
            [strip[i, :, columns] for i in range(A)], axis=0
        )
        for dx in range(1, X):
            copy(("x", dx), (0, 0, dx, 0), here, h)
        for db in range(1, B):
            copy(("b", db), (0, db, 0, 0), here, h)

    def cross(h):
        for dx in range(1, X):
            at = back((0, 0, dx, 0))
            arrive(("x", dx), (0, 0, dx, 0), at, h)
            for db in range(1, B):
                copy(("xb", dx, db), (0, db, 0, 0), at, h, 0)
        for db in range(1, B):
            at = back((0, db, 0, 0))
            arrive(("b", db), (0, db, 0, 0), at, h)
            for dx in range(1, X):
                copy(("bx", dx, db), (0, 0, dx, 0), at, h, 1)
        to_cores(0, h)

    def corner(h):
        for dx in range(1, X):
            for db in range(1, B):
                at = back((0, db, dx, 0))
                arrive(("xb", dx, db), (0, db, 0, 0), at, h, 0)
                arrive(("bx", dx, db), (0, 0, dx, 0), at, h, 1)
            to_cores(dx, h)

    def from_cores(h):
        if C > 1:
            part = rows.at[pl.ds(0, groups // C * (C - 1)), :, pl.ds(0, share_width)]
            pltpu.make_async_copy(part, part, core_sem.at[h]).wait()

    dims_nt = (((1,), (1,)), ((), ()))

    def multiply(k):
        columns = pl.ds(k * step_width, step_width)

        def tile_of(n):
            mine = rows[pl.ds(n * bundle, bundle), :, columns].reshape(tile, step_width)
            place = pl.ds(n * tile if isinstance(n, int) else pl.multiple_of(n * tile, tile), tile)
            for head, total in ((wp, plog_acc), (wr, rlog_acc)):
                logits = lax.dot_general(
                    head[:, columns], mine, dims_nt, preferred_element_type=jnp.float32
                )
                if k == 0:
                    total[:, place] = logits
                else:
                    total[:, place] += logits

        if tokens == tile:
            tile_of(0)
        else:
            pl.loop(0, tokens // tile)(tile_of)

    for h in range(PARTS):
        send_strip(h)
    wanted = to_groups(tgt[...], A, B, piece)
    own.wait()
    for u in range(PARTS + 1):
        if u < PARTS:
            fan(u)
        if 1 <= u:
            cross(u - 1)
        if 2 <= u:
            corner(u - 2)
    load_p.wait()
    load_r.wait()
    early = (PARTS - 1) * STEPS
    for k in range(PARTS * STEPS):
        if k == (early + 1) // 2:
            corner(PARTS - 1)
        if k % STEPS == 0:
            from_cores(k // STEPS)
        multiply(k)

    offset = (v * section + s) * count
    moments = []
    for n in range(tokens // tile):
        place = slice(n * tile, (n + 1) * tile)
        plog, rlog = plog_acc[:, place], rlog_acc[:, place]
        top = jnp.max(plog, axis=0, keepdims=True)
        shift = plog - top
        weight = jnp.exp(shift)
        total = jnp.sum(weight, axis=0, keepdims=True)
        first = jnp.sum(weight * plog, axis=0, keepdims=True)
        across = jnp.sum(weight * (plog - rlog), axis=0, keepdims=True)
        ids = offset + lax.broadcasted_iota(jnp.int32, plog.shape, 0)
        chosen = jnp.sum(jnp.where(ids == wanted[:, place], plog, 0.0), axis=0, keepdims=True)
        rtop = jnp.max(rlog, axis=0, keepdims=True)
        rtotal = jnp.sum(jnp.exp(rlog - rtop), axis=0, keepdims=True)
        none = jnp.zeros_like(top)
        moments.append(
            jnp.concatenate(
                [total, first, across, rtotal, chosen, top, rtop, none], axis=0
            )
        )
    index = b * (X * C) + x * C + c
    plane[index] = jnp.concatenate(moments, axis=1) if len(moments) > 1 else moments[0]

    def exchange(i, steps, buffer, position):
        part = buffer.at[position]
        for step in steps:
            pltpu.make_async_remote_copy(
                src_ref=part, dst_ref=part, send_sem=stat_sent.at[i], recv_sem=stat_sem.at[i],
                device_id=device(to(step)), device_id_type=MESH,
            ).start()

    def exchanged(i, steps, buffer, sem):
        if steps:
            part = buffer.at[pl.ds(0, len(steps))]
            pltpu.make_async_copy(part, part, sem.at[i]).wait()

    exchange(0, plane_steps, plane, index)
    if A > 1:
        sent = strip.at[pl.ds(0, A - 1)]
        pltpu.make_async_copy(sent, sent, strip_sent.at[0]).wait()
    if groups > 1:
        sent = rows.at[pl.ds(0, groups - 1)]
        pltpu.make_async_copy(sent, sent, rows_sent.at[0]).wait()
    exchanged(0, plane_steps, plane, stat_sem)
    line[a] = merge(plane)
    exchange(1, line_steps, line, a)
    exchanged(0, plane_steps, plane, stat_sent)
    exchanged(1, line_steps, line, stat_sem)
    out[...] = merge(line)
    exchanged(1, line_steps, line, stat_sent)


def finish(A, B, stats, msk, out_lp, out_kl, out_tot):
    micro, span = msk.shape
    ordered = from_groups(stats[...], micro, A, B, span // (A * B))
    total, first, across, rtotal, chosen, top, rtop = [ordered[i : i + 1, :] for i in range(7)]
    lse = top + jnp.log(total)
    logprob = chosen - lse
    entropy = lse - first / total
    divergence = across / total - lse + (rtop + jnp.log(rtotal))
    mask = jnp.concatenate([msk[i : i + 1, :] for i in range(micro)], axis=1).astype(jnp.float32)
    scale = 1.0 / (micro * span)
    out_tot[0] = jnp.sum(mask * logprob) * scale
    out_tot[1] = jnp.sum(mask * entropy) * scale
    out_tot[2] = jnp.sum(mask * divergence) * scale
    for i in range(micro):
        out_lp[i : i + 1, :] = logprob[:, i * span : (i + 1) * span]
        out_kl[i : i + 1, :] = divergence[:, i * span : (i + 1) * span]


def on_device(sizes, hidden, policy_head, reference_head, targets, loss_mask):
    vocab, section = sizes
    A, B = split_axis(vocab)
    X, C = split_axis(section)
    piece, width = hidden.shape[1], hidden.shape[2]
    tokens = targets.size
    gathers = (X - 1) + (B - 1) + 2 * (X - 1) * (B - 1)
    anywhere = pl.BlockSpec(memory_space=pl.ANY)
    vmem = pl.BlockSpec(memory_space=pltpu.VMEM)
    heads = policy_head.size + reference_head.size
    moments = pl.pallas_call(
        functools.partial(kernel, sizes),
        out_shape=jax.ShapeDtypeStruct((8, tokens), jnp.float32),
        in_specs=[anywhere, anywhere, anywhere, vmem],
        out_specs=vmem,
        scratch_shapes=[
            pltpu.VMEM((A, piece, width), hidden.dtype),
            pltpu.VMEM((B * X * C, A * piece, width), hidden.dtype),
            pltpu.VMEM(policy_head.shape, policy_head.dtype),
            pltpu.VMEM(reference_head.shape, reference_head.dtype),
            pltpu.VMEM((policy_head.shape[0], tokens), jnp.float32),
            pltpu.VMEM((reference_head.shape[0], tokens), jnp.float32),
            pltpu.VMEM((B * X * C, 8, tokens), jnp.float32),
            pltpu.VMEM((A, 8, tokens), jnp.float32),
            pltpu.SemaphoreType.DMA((3,)),
            pltpu.SemaphoreType.DMA((1,)),
            pltpu.SemaphoreType.DMA((PARTS,)),
            pltpu.SemaphoreType.DMA((1,)),
            pltpu.SemaphoreType.DMA((PARTS,)),
            pltpu.SemaphoreType.DMA((PARTS * gathers,)),
            pltpu.SemaphoreType.DMA((2,)),
            pltpu.SemaphoreType.DMA((2,)),
        ],
        compiler_params=pltpu.CompilerParams(
            collective_id=0, has_side_effects=True, vmem_limit_bytes=60 * 1024 * 1024
        ),
        cost_estimate=pl.CostEstimate(
            flops=2 * tokens * heads, bytes_accessed=2 * heads, transcendentals=3 * tokens * policy_head.shape[0]
        ),
    )(hidden, policy_head, reference_head, targets)
    return pl.pallas_call(
        functools.partial(finish, A, B),
        out_shape=(
            jax.ShapeDtypeStruct(targets.shape, jnp.float32),
            jax.ShapeDtypeStruct(targets.shape, jnp.float32),
            jax.ShapeDtypeStruct((3,), jnp.float32),
        ),
        in_specs=[vmem, vmem],
        out_specs=(vmem, vmem, pl.BlockSpec(memory_space=pltpu.SMEM)),
    )(moments, loss_mask)


def solution(mesh):
    placed = (
        P("section", "vocab", None),
        P(("vocab", "section"), None),
        P(("vocab", "section"), None),
        P(),
        P(),
    )
    sizes = (mesh.shape["vocab"], mesh.shape["section"])
    return jax.shard_map(
        functools.partial(on_device, sizes),
        mesh=mesh, in_specs=placed, out_specs=(P(), P(), P()), check_vma=False,
    )
```

```python
import functools
import itertools

import jax
import jax.numpy as jnp
from jax import lax
from jax.experimental import pallas as pl
from jax.experimental.pallas import tpu as pltpu
from jax.sharding import PartitionSpec as P

MESH = pl.DeviceIdType.MESH


def split_axis(size):
    return (size // 2, 2) if size % 2 == 0 else (size, 1)


def power_of_two(size):
    return size & (size - 1) == 0


def flip(index, step, size):
    result = index
    bit = 1
    while bit < size:
        if step & bit:
            result = result + bit - 2 * bit * lax.rem(lax.div(index, bit), 2)
        bit *= 2
    return result


def target_of(index, step, size):
    if step == 0:
        return index
    return flip(index, step, size) if power_of_two(size) else lax.rem(index + step, size)


def source_of(index, step, size):
    if step == 0:
        return index
    return flip(index, step, size) if power_of_two(size) else lax.rem(index + size - step, size)


def merge(buffer):
    parts = range(buffer.shape[0])
    top = functools.reduce(jnp.maximum, [buffer[i, 5:6, :] for i in parts])
    rtop = functools.reduce(jnp.maximum, [buffer[i, 6:7, :] for i in parts])
    row = lax.broadcasted_iota(jnp.int32, buffer.shape[1:], 0)
    total = jnp.zeros(buffer.shape[1:], buffer.dtype)
    for i in parts:
        shift = jnp.where(row == 3, buffer[i, 6:7, :] - rtop, 0.0)
        shift = jnp.where(row < 3, buffer[i, 5:6, :] - top, shift)
        total = total + jnp.exp(shift) * buffer[i]
    return jnp.where(row == 5, top, jnp.where(row == 6, rtop, total))


def to_groups(values, A, B, piece):
    return jnp.concatenate(
        [
            values[m : m + 1, (i * B + j) * piece : (i * B + j + 1) * piece]
            for m in range(values.shape[0]) for j in range(B) for i in range(A)
        ],
        axis=1,
    )


def from_groups(values, micro, A, B, piece):
    starts = [((m * B + j) * A + i) * piece for m in range(micro) for i in range(A) for j in range(B)]
    return jnp.concatenate([values[:, at : at + piece] for at in starts], axis=1)


PARTS = 2
STEPS = 2


def kernel(
    sizes, hid, hp, hr, tgt, out,
    strip, rows, wp, wr, plog_acc, rlog_acc, plane, line,
    local_sem, strip_sent, strip_sem, rows_sent, core_sem, recv_sem, stat_sent, stat_sem,
):
    vocab, section = sizes
    A, B = split_axis(vocab)
    X, C = split_axis(section)
    v, s = lax.axis_index("vocab"), lax.axis_index("section")
    a, b = lax.div(v, B), lax.rem(v, B)
    x, c = lax.div(s, C), lax.rem(s, C)
    dims = (A, B, X, C)
    here = (a, b, x, c)
    piece, width = hid.shape[1], hid.shape[2]
    groups, high = rows.shape[0], rows.shape[1]
    tokens = groups * high
    count = wp.shape[0]
    share_width = width // PARTS
    step_width = share_width // STEPS
    bundle = 128 // high if tokens % 128 == 0 and 128 % high == 0 else groups
    tile = bundle * high

    def device(at):
        return (at[0] * B + at[1], at[2] * C + at[3])

    def group(at):
        return (at[2] * C + at[3]) * B + at[1]

    outward = [[target_of(i, d, n) for d in range(n)] for i, n in zip(here, dims)]
    inward = [[source_of(i, d, n) for d in range(n)] for i, n in zip(here, dims)]

    def to(step):
        return tuple(known[d] for known, d in zip(outward, step))

    def back(step):
        return tuple(known[d] for known, d in zip(inward, step))

    own = pltpu.make_async_copy(hid.at[0], strip.at[a], local_sem.at[0])
    own.start()
    line_steps = [(d, 0, 0, 0) for d in range(1, A)]
    plane_steps = [(0,) + e for e in itertools.product(range(B), range(X), range(C)) if any(e)]
    barrier = pltpu.get_barrier_semaphore()
    for step in line_steps + plane_steps:
        pl.semaphore_signal(barrier, inc=1, device_id=device(to(step)), device_id_type=MESH)

    load_p = pltpu.make_async_copy(hp, wp, local_sem.at[1])
    load_p.start()
    load_r = pltpu.make_async_copy(hr, wr, local_sem.at[2])
    load_r.start()
    pl.semaphore_wait(barrier, len(line_steps) + len(plane_steps))

    keys = {}

    def view(at, h, half):
        lo, size = h * share_width, share_width
        if half is not None:
            size = share_width // 2
            lo = lo + half * size
        return rows.at[group(at), :, pl.ds(lo, size)]

    def describe(key, step, at, h, half):
        part = view(at, h, half)
        arrived = recv_sem.at[keys.setdefault((h,) + key, len(keys))]
        return pltpu.make_async_remote_copy(
            src_ref=part, dst_ref=part, send_sem=rows_sent.at[0], recv_sem=arrived,
            device_id=device(to(step)), device_id_type=MESH,
        )

    def copy(key, step, at, h, half=None):
        describe(key, step, at, h, half).start()

    def arrive(key, step, at, h, half=None):
        describe(key, step, at, h, half).wait_recv()

    def to_cores(dx, h):
        first = (back((0, 0, dx, 0))[2] * C + c) * B
        part = rows.at[pl.ds(first, B), :, pl.ds(h * share_width, share_width)]
        for dc in range(1, C):
            pltpu.make_async_remote_copy(
                src_ref=part, dst_ref=part, send_sem=rows_sent.at[0], recv_sem=core_sem.at[h],
                device_id=device(to((0, 0, 0, dc))), device_id_type=MESH,
            ).start()

    def send_strip(h):
        columns = pl.ds(h * share_width, share_width)
        for step in line_steps:
            pltpu.make_async_remote_copy(
                src_ref=hid.at[0, :, columns], dst_ref=strip.at[a, :, columns], send_sem=strip_sent.at[0], recv_sem=strip_sem.at[h],
                device_id=device(to(step)), device_id_type=MESH,
            ).start()

    def fan(h):
        columns = pl.ds(h * share_width, share_width)
        if A > 1:
            part = strip.at[pl.ds(0, A - 1), :, columns]
            pltpu.make_async_copy(part, part, strip_sem.at[h]).wait()
        rows[group(here), :, columns] = jnp.concatenate(
            [strip[i, :, columns] for i in range(A)], axis=0
        )
        for dx in range(1, X):
            copy(("x", dx), (0, 0, dx, 0), here, h)
        for db in range(1, B):
            copy(("b", db), (0, db, 0, 0), here, h)

    def cross(h):
        for dx in range(1, X):
            at = back((0, 0, dx, 0))
            arrive(("x", dx), (0, 0, dx, 0), at, h)
            for db in range(1, B):
                copy(("xb", dx, db), (0, db, 0, 0), at, h, 0)
        for db in range(1, B):
            at = back((0, db, 0, 0))
            arrive(("b", db), (0, db, 0, 0), at, h)
            for dx in range(1, X):
                copy(("bx", dx, db), (0, 0, dx, 0), at, h, 1)
        to_cores(0, h)

    def corner(h):
        for dx in range(1, X):
            for db in range(1, B):
                at = back((0, db, dx, 0))
                arrive(("xb", dx, db), (0, db, 0, 0), at, h, 0)
                arrive(("bx", dx, db), (0, 0, dx, 0), at, h, 1)
            to_cores(dx, h)

    def from_cores(h):
        if C > 1:
            part = rows.at[pl.ds(0, groups // C * (C - 1)), :, pl.ds(0, share_width)]
            pltpu.make_async_copy(part, part, core_sem.at[h]).wait()

    dims_nt = (((1,), (1,)), ((), ()))

    def multiply(k):
        columns = pl.ds(k * step_width, step_width)

        def tile_of(n):
            mine = rows[pl.ds(n * bundle, bundle), :, columns].reshape(tile, step_width)
            place = pl.ds(n * tile if isinstance(n, int) else pl.multiple_of(n * tile, tile), tile)
            for head, total in ((wp, plog_acc), (wr, rlog_acc)):
                logits = lax.dot_general(
                    head[:, columns], mine, dims_nt, preferred_element_type=jnp.float32
                )
                if k == 0:
                    total[:, place] = logits
                else:
                    total[:, place] += logits

        if tokens == tile:
            tile_of(0)
        else:
            pl.loop(0, tokens // tile)(tile_of)

    for h in range(PARTS):
        send_strip(h)
    wanted = to_groups(tgt[...], A, B, piece)
    own.wait()
    for u in range(PARTS + 1):
        if u < PARTS:
            fan(u)
        if 1 <= u:
            cross(u - 1)
        if 2 <= u:
            corner(u - 2)
    load_p.wait()
    load_r.wait()
    early = (PARTS - 1) * STEPS
    for k in range(PARTS * STEPS):
        if k == (early + 1) // 2:
            corner(PARTS - 1)
        if k % STEPS == 0:
            from_cores(k // STEPS)
        multiply(k)

    offset = (v * section + s) * count
    moments = []
    for n in range(tokens // tile):
        place = slice(n * tile, (n + 1) * tile)
        plog, rlog = plog_acc[:, place], rlog_acc[:, place]
        top = jnp.max(plog, axis=0, keepdims=True)
        shift = plog - top
        weight = jnp.exp(shift)
        total = jnp.sum(weight, axis=0, keepdims=True)
        first = jnp.sum(weight * plog, axis=0, keepdims=True)
        across = jnp.sum(weight * (plog - rlog), axis=0, keepdims=True)
        ids = offset + lax.broadcasted_iota(jnp.int32, plog.shape, 0)
        chosen = jnp.sum(jnp.where(ids == wanted[:, place], plog, 0.0), axis=0, keepdims=True)
        rtop = jnp.max(rlog, axis=0, keepdims=True)
        rtotal = jnp.sum(jnp.exp(rlog - rtop), axis=0, keepdims=True)
        none = jnp.zeros_like(top)
        moments.append(
            jnp.concatenate(
                [total, first, across, rtotal, chosen, top, rtop, none], axis=0
            )
        )
    index = b * (X * C) + x * C + c
    plane[index] = jnp.concatenate(moments, axis=1) if len(moments) > 1 else moments[0]

    def exchange(i, steps, buffer, position):
        part = buffer.at[position]
        for step in steps:
            pltpu.make_async_remote_copy(
                src_ref=part, dst_ref=part, send_sem=stat_sent.at[i], recv_sem=stat_sem.at[i],
                device_id=device(to(step)), device_id_type=MESH,
            ).start()

    def exchanged(i, steps, buffer, sem):
        if steps:
            part = buffer.at[pl.ds(0, len(steps))]
            pltpu.make_async_copy(part, part, sem.at[i]).wait()

    exchange(0, plane_steps, plane, index)
    if A > 1:
        sent = strip.at[pl.ds(0, A - 1)]
        pltpu.make_async_copy(sent, sent, strip_sent.at[0]).wait()
    if groups > 1:
        sent = rows.at[pl.ds(0, groups - 1)]
        pltpu.make_async_copy(sent, sent, rows_sent.at[0]).wait()
    exchanged(0, plane_steps, plane, stat_sem)
    line[a] = merge(plane)
    exchange(1, line_steps, line, a)
    exchanged(0, plane_steps, plane, stat_sent)
    exchanged(1, line_steps, line, stat_sem)
    out[...] = merge(line)
    exchanged(1, line_steps, line, stat_sent)


def finish(A, B, stats, msk, out_lp, out_kl, out_tot):
    micro, span = msk.shape
    ordered = from_groups(stats[...], micro, A, B, span // (A * B))
    total, first, across, rtotal, chosen, top, rtop = [ordered[i : i + 1, :] for i in range(7)]
    lse = top + jnp.log(total)
    logprob = chosen - lse
    entropy = lse - first / total
    divergence = across / total - lse + (rtop + jnp.log(rtotal))
    mask = jnp.concatenate([msk[i : i + 1, :] for i in range(micro)], axis=1).astype(jnp.float32)
    scale = 1.0 / (micro * span)
    out_tot[0] = jnp.sum(mask * logprob) * scale
    out_tot[1] = jnp.sum(mask * entropy) * scale
    out_tot[2] = jnp.sum(mask * divergence) * scale
    for i in range(micro):
        out_lp[i : i + 1, :] = logprob[:, i * span : (i + 1) * span]
        out_kl[i : i + 1, :] = divergence[:, i * span : (i + 1) * span]


def on_device(sizes, hidden, policy_head, reference_head, targets, loss_mask):
    vocab, section = sizes
    A, B = split_axis(vocab)
    X, C = split_axis(section)
    piece, width = hidden.shape[1], hidden.shape[2]
    tokens = targets.size
    gathers = (X - 1) + (B - 1) + 2 * (X - 1) * (B - 1)
    anywhere = pl.BlockSpec(memory_space=pl.ANY)
    vmem = pl.BlockSpec(memory_space=pltpu.VMEM)
    heads = policy_head.size + reference_head.size
    moments = pl.pallas_call(
        functools.partial(kernel, sizes),
        out_shape=jax.ShapeDtypeStruct((8, tokens), jnp.float32),
        in_specs=[anywhere, anywhere, anywhere, vmem],
        out_specs=vmem,
        scratch_shapes=[
            pltpu.VMEM((A, piece, width), hidden.dtype),
            pltpu.VMEM((B * X * C, A * piece, width), hidden.dtype),
            pltpu.VMEM(policy_head.shape, policy_head.dtype),
            pltpu.VMEM(reference_head.shape, reference_head.dtype),
            pltpu.VMEM((policy_head.shape[0], tokens), jnp.float32),
            pltpu.VMEM((reference_head.shape[0], tokens), jnp.float32),
            pltpu.VMEM((B * X * C, 8, tokens), jnp.float32),
            pltpu.VMEM((A, 8, tokens), jnp.float32),
            pltpu.SemaphoreType.DMA((3,)),
            pltpu.SemaphoreType.DMA((1,)),
            pltpu.SemaphoreType.DMA((PARTS,)),
            pltpu.SemaphoreType.DMA((1,)),
            pltpu.SemaphoreType.DMA((PARTS,)),
            pltpu.SemaphoreType.DMA((PARTS * gathers,)),
            pltpu.SemaphoreType.DMA((2,)),
            pltpu.SemaphoreType.DMA((2,)),
        ],
        compiler_params=pltpu.CompilerParams(
            collective_id=0, has_side_effects=True, vmem_limit_bytes=60 * 1024 * 1024
        ),
        cost_estimate=pl.CostEstimate(
            flops=2 * tokens * heads, bytes_accessed=2 * heads, transcendentals=3 * tokens * policy_head.shape[0]
        ),
    )(hidden, policy_head, reference_head, targets)
    return pl.pallas_call(
        functools.partial(finish, A, B),
        out_shape=(
            jax.ShapeDtypeStruct(targets.shape, jnp.float32),
            jax.ShapeDtypeStruct(targets.shape, jnp.float32),
            jax.ShapeDtypeStruct((3,), jnp.float32),
        ),
        in_specs=[vmem, vmem],
        out_specs=(vmem, vmem, pl.BlockSpec(memory_space=pltpu.SMEM)),
    )(moments, loss_mask)


def solution(mesh):
    placed = (
        P("section", "vocab", None),
        P(("vocab", "section"), None),
        P(("vocab", "section"), None),
        P(),
        P(),
    )
    sizes = (mesh.shape["vocab"], mesh.shape["section"])
    return jax.shard_map(
        functools.partial(on_device, sizes),
        mesh=mesh, in_specs=placed, out_specs=(P(), P(), P()), check_vma=False,
    )
```
